128 devices in a mesh: section: 4 (over y), tp: 32 (over z, x, core).
Axes of the slice: x: 4, y: 4, z: 4, core: 2. Of those that a mesh axis runs over, the one named last changes fastest.
Arguments:
- forward_inputs: bfloat16 [4, 1024, 8192], P('section', None, 'tp'), may hold values from -6 to 6
- backward_inputs: bfloat16 [4, 1024, 8192], P('section', None, 'tp'), may hold values from -6 to 6
- backward_cotangents: bfloat16 [4, 1024, 8192], P('section', None, 'tp'), may hold values from -0.75 to 0.75
- frozen_weight: bfloat16 [4, 8192, 8192], P('section', None, 'tp'), may hold values from -0.125 to 0.125
- adapter_down_weight: bfloat16 [4, 64, 8192, 128], P('section', 'tp'), may hold values from -0.0625 to 0.0625
- adapter_up_weight: bfloat16 [4, 64, 128, 8192], P('section', 'tp'), may hold values from -0.5 to 0.5
- forward_counts: int32 [4, 64], P('section'), may hold values from 1 to 32, 1024 in all within a row
- backward_counts: int32 [4, 64], P('section'), may hold values from 1 to 32, 1024 in all within a row
- ranks: int32 [64], replicated, may hold values from 16 to 128, as said below
- adapter_slot: int32 [64], replicated, may hold values from 0 to 63, each once
Outputs:
- next_fwd: bfloat16 [4, 1024, 8192], P('section', None, 'tp')
- next_bwd: bfloat16 [4, 1024, 8192], P('section', None, 'tp')
- grad_a: bfloat16 [4, 64, 8192, 128], P('section', 'tp')
- grad_b: bfloat16 [4, 64, 128, 8192], P('section', 'tp')
The draws below stay inside these ranges and needn't reach their ends.
Inputs may be any that keep to these rules, and one draw needn't show every extreme that they name: `forward_counts`: each section's row sums to 1024; its largest entry is exactly 32. `backward_counts`: each section's row sums to 1024; its largest entry is exactly 32. `ranks`: some adapter has rank 128 and some other has the least rank. `adapter_slot`: A permutation: slot k of the adapter dimension lies on device k // 2 of tp.
All inputs are finite; a program needn't handle non-finite values.
Results may differ from the reference program's by a relative error of at most 0.005.
Values may be sent and summed in bfloat16 or wider, within the bound.
No kernel may reach another device: no remote copies, remote signals or barrier semaphores. Data moves between devices by JAX's collectives and lax.ppermute only.
A program may use at most 192 MiB of HBM per device.

```python
import math
import jax
import jax.numpy as jnp
import numpy as np
from jax import lax

MODEL_DIM = 8192
TOKENS = 1024
LARGEST_RANK = 128
ADAPTER_COUNT = 64
MOST = 32
SECTION_COUNT = 4
N_SECTION = 4


def draw_ranks(key, part):
    key = jax.random.fold_in(key, 11)
    key_base, key_first, key_step = jax.random.split(key, 3)
    values = jax.random.randint(key_base, (ADAPTER_COUNT,), LARGEST_RANK // 8, LARGEST_RANK + 1, dtype=jnp.int32)
    first_pick = jax.random.randint(key_first, (), 0, ADAPTER_COUNT, dtype=jnp.int32)
    step_pick = jax.random.randint(key_step, (), 1, ADAPTER_COUNT, dtype=jnp.int32)
    second_pick = (first_pick + step_pick) % ADAPTER_COUNT
    values = values.at[first_pick].set(LARGEST_RANK)
    values = values.at[second_pick].set(LARGEST_RANK // 8)
    return values.astype(jnp.int32)


def with_spikes(values, key, source, target, shards_of, factor):
    owner, partner = [(jnp.arange(values.shape[position]) // (values.shape[position] // shards_of)).reshape([-1 if axis == position else 1 for axis in range(values.ndim)]) for position in (source, target)]
    chosen = jax.random.permutation(key, shards_of)[partner]
    strong = (owner == chosen) | (owner == (partner + shards_of // 2) % shards_of)
    return jnp.where(strong, factor * values, values)


def level_of(rng, shape, pieces, low, largest):
    factor_of = 1.0
    for position, blocks in pieces:
        heights = jax.random.uniform(jax.random.fold_in(jax.random.fold_in(rng, 6), position), (blocks,), jnp.float32, low / len(pieces), largest / len(pieces))
        factor_of = factor_of * jnp.repeat(jnp.exp(heights), shape[position] // blocks).reshape((-1,) + (1,) * (len(shape) - 1 - position))
    return factor_of


def length_profile(amount, total, most, skew):
    loads = [(1 << 20) // math.isqrt(standing ** skew) + 1 for standing in range(2, amount + 1)]
    surplus, holding = total - most - (amount - 1), [1] * (amount - 1)
    while surplus > 0:
        movable = [i for i in range(amount - 1) if holding[i] < most]
        mass, budget = sum([loads[i] for i in movable]), surplus
        for i in movable:
            extra = min(most - holding[i], max(1, budget * loads[i] // mass), surplus)
            holding[i] = holding[i] + extra
            surplus = surplus - extra
    return np.array([most] + holding)


def uneven_parts(rng, count, total, reach, skew):
    if count == 2:
        one = jax.random.randint(rng, (), max(1, total - reach), min(reach, total - 1) + 1)
        return jnp.stack([one, total - one])
    sizes = jnp.asarray(length_profile(count, total, reach, skew), jnp.int32)
    pairs = (count - 1) // 2
    donor, receiver = sizes[1:1 + 2 * pairs:2], sizes[2:2 + 2 * pairs:2]
    slack = jnp.minimum(donor - 1, reach - receiver)
    moved = jax.random.randint(jax.random.fold_in(rng, 1), (pairs,), 0, 1 << 20) % (slack + 1)
    sizes = sizes.at[1:1 + 2 * pairs:2].set(donor - moved).at[2:2 + 2 * pairs:2].set(receiver + moved)
    return sizes[jax.random.permutation(jax.random.fold_in(rng, 2), count)]


def centred(key, shape, scale, most, shards=(), held_as=jnp.bfloat16):
    values = jax.random.normal(key, shape, jnp.float32) * scale
    if len(shards) > 0:
        values = level_of(key, shape, shards, -0.22, 0.18) * values
    return jnp.clip(values, min=-most, max=most).astype(held_as)


def heavy_noise(own_key, extent, deviation, reach, pieces, heavy, kind=jnp.bfloat16):
    values = deviation * jax.random.normal(own_key, extent, jnp.float32)
    if pieces:
        values = values * level_of(own_key, extent, pieces, -0.22, 0.18)
    return jnp.clip(with_spikes(values, jax.random.fold_in(own_key, 3), *heavy), -reach, reach).astype(kind)


def setup_inputs(seed: int = 0) -> dict:
    streams_of = jax.random.split(jax.random.key(seed), 11)
    forward_inputs = centred(streams_of[0], (SECTION_COUNT, TOKENS, MODEL_DIM), 1.0, 6.0, ((0, 4), (2, 32)))
    backward_inputs = centred(streams_of[1], (SECTION_COUNT, TOKENS, MODEL_DIM), 1.0, 6.0, ((0, 4), (2, 32)))
    backward_cotangents = centred(streams_of[2], (SECTION_COUNT, TOKENS, MODEL_DIM), 0.125, 0.75, ((0, 4), (2, 32)))
    frozen_weight = heavy_noise(streams_of[3], (SECTION_COUNT, MODEL_DIM, MODEL_DIM), MODEL_DIM ** -0.5, 0.125, ((0, 4), (2, 32)), (2, 1, 32, 2.75))
    adapter_down_weight = centred(streams_of[4], (SECTION_COUNT, ADAPTER_COUNT, MODEL_DIM, LARGEST_RANK), MODEL_DIM ** -0.5, 0.0625, ((0, 4), (1, 32)))
    adapter_up_weight = centred(streams_of[5], (SECTION_COUNT, ADAPTER_COUNT, LARGEST_RANK, MODEL_DIM), LARGEST_RANK ** -0.5, 0.5, ((0, 4), (1, 32)))
    forward_counts = jax.vmap(lambda own: uneven_parts(own, ADAPTER_COUNT, TOKENS, MOST, 2))(jax.random.split(streams_of[6], SECTION_COUNT)).reshape((SECTION_COUNT, ADAPTER_COUNT)).astype(jnp.int32)
    backward_counts = jax.vmap(lambda own: uneven_parts(own, ADAPTER_COUNT, TOKENS, MOST, 2))(jax.random.split(streams_of[7], SECTION_COUNT)).reshape((SECTION_COUNT, ADAPTER_COUNT)).astype(jnp.int32)
    ranks = draw_ranks(jax.random.fold_in(streams_of[10], 71), 0)
    adapter_slot = jax.random.permutation(streams_of[9], ADAPTER_COUNT).astype(jnp.int32)
    return {"forward_inputs": forward_inputs, "backward_inputs": backward_inputs, "backward_cotangents": backward_cotangents, "frozen_weight": frozen_weight, "adapter_down_weight": adapter_down_weight, "adapter_up_weight": adapter_up_weight, "forward_counts": forward_counts, "backward_counts": backward_counts, "ranks": ranks, "adapter_slot": adapter_slot}


def layout(counts, ranks, adapter_slot):
    end_rows = jnp.cumsum(counts)
    starts = end_rows - counts
    token_ids = jnp.arange(TOKENS, dtype=jnp.int32)
    token_adapter = lax.optimization_barrier(jnp.sum((end_rows[None, :] <= token_ids[:, None]).astype(jnp.int32), axis=1)).astype(jnp.int32)
    begins = jnp.minimum(starts, TOKENS - MOST).astype(jnp.int32)
    adapter_ids = jnp.arange(ADAPTER_COUNT, dtype=jnp.int32)
    adapter_of_slot = jnp.zeros((ADAPTER_COUNT,), jnp.int32).at[adapter_slot].set(adapter_ids)
    slot_begin = begins[adapter_of_slot]
    slot_start = starts[adapter_of_slot]
    slot_length = counts[adapter_of_slot]
    slot_rank = ranks[adapter_of_slot]
    offsets = jnp.arange(MOST, dtype=jnp.int32)
    positions = slot_begin[:, None] + offsets[None, :]
    inside = (positions >= slot_start[:, None]) & (positions < (slot_start + slot_length)[:, None])
    rank_ids = jnp.arange(LARGEST_RANK, dtype=jnp.int32)
    alive = inside[:, :, None] & (rank_ids[None, None, :] < slot_rank[:, None, None])
    factor = 8.0 / jnp.sqrt(slot_rank.astype(jnp.float32))
    weights = jnp.where(alive, factor[:, None, None], jnp.zeros((), jnp.float32))
    token_slot = adapter_slot[token_adapter]
    token_place = (token_slot * MOST + token_ids - begins[token_adapter]).astype(jnp.int32)
    return (positions.reshape(-1).astype(jnp.int32), token_place, weights)

def reference(forward_inputs, backward_inputs, backward_cotangents, frozen_weight, adapter_down_weight, adapter_up_weight, forward_counts, backward_counts, ranks, adapter_slot):
    forward_out = []
    backward_out = []
    grads_down = []
    grads_up = []
    for layer_number in range(N_SECTION):
        weight = frozen_weight[layer_number]
        down_matrix = adapter_down_weight[layer_number].astype(jnp.float32)
        up_matrix = adapter_up_weight[layer_number].astype(jnp.float32)
        positions, token_place, weights = layout(forward_counts[layer_number], ranks, adapter_slot)
        inputs = forward_inputs[layer_number]
        window_rows = inputs[positions].reshape(ADAPTER_COUNT, MOST, MODEL_DIM).astype(jnp.float32)
        code_rows = (jnp.einsum('amd,adr->amr', window_rows, down_matrix) * weights).astype(jnp.bfloat16)
        adapter_out = jnp.einsum('amr,ard->amd', code_rows.astype(jnp.float32), up_matrix).astype(jnp.bfloat16)
        adapter_rows = adapter_out.reshape(ADAPTER_COUNT * MOST, MODEL_DIM)[token_place]
        base_out = jnp.dot(inputs, weight, preferred_element_type=jnp.float32)
        forward_out.append((inputs.astype(jnp.float32) + base_out + adapter_rows.astype(jnp.float32)).astype(jnp.bfloat16))
        positions, token_place, weights = layout(backward_counts[layer_number], ranks, adapter_slot)
        stash = backward_inputs[layer_number]
        cotangent = backward_cotangents[layer_number]
        stash_rows = stash[positions].reshape(ADAPTER_COUNT, MOST, MODEL_DIM).astype(jnp.float32)
        grad_rows = cotangent[positions].reshape(ADAPTER_COUNT, MOST, MODEL_DIM).astype(jnp.float32)
        back_codes = (jnp.einsum('amd,adr->amr', stash_rows, down_matrix) * weights).astype(jnp.bfloat16)
        code_grads = (jnp.einsum('amd,ard->amr', grad_rows, up_matrix) * weights).astype(jnp.bfloat16)
        grads_up.append(jnp.einsum('amr,amd->ard', back_codes.astype(jnp.float32), grad_rows).astype(jnp.bfloat16))
        grads_down.append(jnp.einsum('amd,amr->adr', stash_rows, code_grads.astype(jnp.float32)).astype(jnp.bfloat16))
        returned = jnp.einsum('amr,adr->amd', code_grads.astype(jnp.float32), down_matrix)
        returned_rows = returned.reshape(ADAPTER_COUNT * MOST, MODEL_DIM)[token_place]
        back_out = jnp.dot(cotangent, weight.T, preferred_element_type=jnp.float32)
        backward_out.append((cotangent.astype(jnp.float32) + back_out + returned_rows).astype(jnp.bfloat16))
    next_fwd = jnp.stack([forward_out[(index_s - 1) % N_SECTION] for index_s in range(N_SECTION)])
    next_bwd = jnp.stack([backward_out[(index_s + 1) % N_SECTION] for index_s in range(N_SECTION)])
    return (next_fwd, next_bwd, jnp.stack(grads_down), jnp.stack(grads_up))
```

```python
import functools

import jax
import jax.numpy as jnp
from jax import lax
from jax.experimental import pallas as pl
from jax.experimental.pallas import tpu as pltpu
from jax.sharding import PartitionSpec as P

BF16 = jnp.bfloat16
F32 = jnp.float32
SIDE = 4
CHIPS = 16
CORES = 2
BLOCK = 256
VMEM = 56 * 1024 * 1024


def place(z, x, core):
    return (z * SIDE + x) * CORES + core


def ring_pairs(first, step):
    pairs = []
    for z in range(SIDE):
        for x in range(SIDE):
            for core in range(CORES):
                along_x = (core == 0) == first
                target = place(z, (x + step) % SIDE, core) if along_x else place((z + step) % SIDE, x, core)
                pairs.append((place(z, x, core), target))
    return pairs


FIRST_UP, FIRST_DOWN = ring_pairs(True, 1), ring_pairs(True, -1)
SECOND_UP, SECOND_DOWN = ring_pairs(False, 1), ring_pairs(False, -1)
OTHER_CORE = [(index, index ^ 1) for index in range(CHIPS * CORES)]
SAME_CORE = [[chip * CORES + core for chip in range(CHIPS)] for core in range(CORES)]


def send(value, pairs):
    return lax.ppermute(value, "tp", pairs)


def shifted(value, axis, steps):
    count = lax.axis_size(axis)
    pairs = [(source, (source + steps) % count) for source in range(count)]
    return lax.ppermute(value, axis, pairs)


def slots(counts, ranks, adapter_slot, window):
    adapters = adapter_slot.shape[0]
    lengths = counts[0]
    ids = jnp.arange(adapters, dtype=jnp.int32)
    starts = jnp.sum(jnp.where(ids[None, :] < ids[:, None], lengths[None, :], 0), axis=1)
    placed = adapter_slot[:, None] == ids[None, :]
    slot_start = jnp.sum(jnp.where(placed, starts[:, None], 0), axis=0)
    slot_length = jnp.sum(jnp.where(placed, lengths[:, None], 0), axis=0)
    slot_rank = jnp.sum(jnp.where(placed, ranks[:, None], 0), axis=0)
    offsets = jnp.arange(window, dtype=jnp.int32)
    token = jnp.where(offsets[None, :] < slot_length[:, None], slot_start[:, None] + offsets[None, :], -1)
    return token.reshape(-1), slot_rank


def forward_body(core_ref, x_ref, own_w_ref, other_w_ref, rows_ref, own_ref, other_ref, window_ref):
    step = pl.program_id(0)

    @pl.when(step == 0)
    def _():
        own_ref[...] = jnp.zeros_like(own_ref)
        other_ref[...] = jnp.zeros_like(other_ref)

    x = x_ref[0]
    own_ref[...] += jnp.dot(x, own_w_ref[0, 0], preferred_element_type=F32)
    other_ref[...] += jnp.dot(x, other_w_ref[0], preferred_element_type=F32)
    window_ref[0] = jnp.dot(rows_ref[...], x, preferred_element_type=F32).astype(BF16)


def forward_product(core, gathered, weight, other_weight, rows):
    tokens = gathered.shape[1]
    return pl.pallas_call(
        forward_body,
        grid_spec=pltpu.PrefetchScalarGridSpec(
            num_scalar_prefetch=1,
            grid=(CHIPS,),
            in_specs=[
                pl.BlockSpec((1, tokens, BLOCK), lambda k, core: (k, 0, 0)),
                pl.BlockSpec((1, 1, BLOCK, BLOCK), lambda k, core: (k, core[0], 0, 0)),
                pl.BlockSpec((1, BLOCK, BLOCK), lambda k, core: (k, 0, 0)),
                pl.BlockSpec(rows.shape, lambda k, core: (0, 0)),
            ],
            out_specs=[
                pl.BlockSpec((tokens, BLOCK), lambda k, core: (0, 0)),
                pl.BlockSpec((tokens, BLOCK), lambda k, core: (0, 0)),
                pl.BlockSpec((1, rows.shape[0], BLOCK), lambda k, core: (k, 0, 0)),
            ],
        ),
        out_shape=[
            jax.ShapeDtypeStruct((tokens, BLOCK), F32),
            jax.ShapeDtypeStruct((tokens, BLOCK), F32),
            jax.ShapeDtypeStruct((CHIPS, rows.shape[0], BLOCK), BF16),
        ],
        compiler_params=pltpu.CompilerParams(vmem_limit_bytes=VMEM),
        cost_estimate=pl.CostEstimate(flops=10 * 10**9, bytes_accessed=16 * 2**20, transcendentals=0),
        name="forward_product",
    )(core, gathered, weight, other_weight, rows)


def backward_body(takes, order_ref, own_g_ref, other_g_ref, own_w_ref, other_w_ref, spread_ref, returned_ref, *rest):
    received, out_ref = rest[:-1], rest[-1]
    step = pl.program_id(0)
    contract = (((1,), (1,)), ((), ()))
    total = lax.dot_general(own_g_ref[...], own_w_ref[0, 0], contract, preferred_element_type=F32)
    total += lax.dot_general(other_g_ref[...], other_w_ref[0], contract, preferred_element_type=F32)
    total += jnp.dot(spread_ref[...], returned_ref[0], preferred_element_type=F32)
    if not received:
        out_ref[0] = total.astype(BF16)
        return
    for ref, (low, high) in zip(received, takes):
        inside = (step >= low) & (step < high)
        total += jnp.where(inside, ref[0].astype(F32), 0.0)
    out_ref[0] = total.astype(BF16)


def backward_product(order, grads, weight, other_weight, spread, returned, received=(), takes=()):
    own_grad, other_grad = grads
    tokens = own_grad.shape[0]
    blocks = order.shape[0] - 1

    def taken(bounds):
        low, high = bounds
        return pl.BlockSpec((1, tokens, BLOCK), lambda j, order: (jnp.clip(j - low, 0, high - low - 1), 0, 0))

    whole = lambda shape: pl.BlockSpec(shape, lambda j, order: (0, 0))
    return pl.pallas_call(
        functools.partial(backward_body, takes),
        grid_spec=pltpu.PrefetchScalarGridSpec(
            num_scalar_prefetch=1,
            grid=(blocks,),
            in_specs=[
                whole((tokens, BLOCK)),
                whole((tokens, BLOCK)),
                pl.BlockSpec((1, 1, BLOCK, BLOCK), lambda j, order: (order[j], order[blocks], 0, 0)),
                pl.BlockSpec((1, BLOCK, BLOCK), lambda j, order: (order[j], 0, 0)),
                whole(spread.shape),
                pl.BlockSpec((1, returned.shape[1], BLOCK), lambda j, order: (order[j], 0, 0)),
            ]
            + [taken(bounds) for bounds in takes],
            out_specs=pl.BlockSpec((1, tokens, BLOCK), lambda j, order: (j, 0, 0)),
        ),
        out_shape=jax.ShapeDtypeStruct((blocks, tokens, BLOCK), BF16),
        compiler_params=pltpu.CompilerParams(vmem_limit_bytes=VMEM),
        cost_estimate=pl.CostEstimate(flops=blocks * 34 * 10**7, bytes_accessed=blocks * 2**20, transcendentals=0),
        name="backward_product",
    )(order, own_grad, other_grad, weight, other_weight, spread, returned, *received)


def add_rounded(*values):
    total = values[0].astype(F32)
    for value in values[1:]:
        total = total + value.astype(F32)
    return total.astype(BF16)


def shards(
    forward_inputs,
    backward_inputs,
    backward_cotangents,
    frozen_weight,
    adapter_down_weight,
    adapter_up_weight,
    forward_counts,
    backward_counts,
    ranks,
    adapter_slot,
):
    tokens = forward_inputs.shape[1]
    adapters = adapter_slot.shape[0]
    owned = adapter_down_weight.shape[1]
    rank = adapter_down_weight.shape[3]
    window = 2 * tokens // adapters
    rows = owned * window
    devices = CHIPS * CORES
    half = tokens // 2
    device = lax.axis_index("tp")
    core = device % CORES
    chip = device // CORES
    chip_z, chip_x = chip // SIDE, chip % SIDE

    layer_in = forward_inputs[0]
    stash = backward_inputs[0]
    cotangent = backward_cotangents[0]
    weight = frozen_weight[0].reshape(CHIPS, CORES, BLOCK, BLOCK)
    down = adapter_down_weight[0]
    up = adapter_up_weight[0]

    gathered = lax.all_gather(layer_in, "tp", axis=0, axis_index_groups=SAME_CORE)

    for_other = lax.dynamic_index_in_dim(weight, 1 - core, axis=1, keepdims=False)
    other_weight = send(for_other, OTHER_CORE)
    other_cotangent = send(cotangent, OTHER_CORE)

    fwd_token, slot_rank = slots(forward_counts, ranks, adapter_slot, window)
    bwd_token, _ = slots(backward_counts, ranks, adapter_slot, window)
    token_ids = jnp.arange(tokens, dtype=jnp.int32)
    own_rank = lax.dynamic_slice_in_dim(slot_rank, device * owned, owned)
    live = jnp.arange(rank, dtype=jnp.int32)[None, :] < own_rank[:, None]
    scale = jnp.where(live, 8.0 / jnp.sqrt(own_rank.astype(F32))[:, None], 0.0)[:, None, :]

    def of_chip(token):
        mine = lax.dynamic_slice_in_dim(token, device * rows, rows)
        other = lax.dynamic_slice_in_dim(token, (device ^ 1) * rows, rows)
        return jnp.concatenate([mine, other])

    pick = (bwd_token[:, None] == token_ids[None, :]).astype(BF16)
    both = jnp.concatenate([stash, cotangent], axis=1)
    windows = jnp.dot(pick, both, preferred_element_type=F32).astype(BF16)
    windows = windows.reshape(devices, rows, CORES * BLOCK)
    windows = lax.all_to_all(windows, "tp", split_axis=0, concat_axis=0, tiled=True)
    windows = windows.reshape(devices, owned, window, 2, BLOCK).transpose(3, 1, 2, 0, 4)
    windows = windows.reshape(2, owned, window, devices * BLOCK)
    stash_rows, grad_rows = windows[0], windows[1]

    back_codes = jnp.einsum("kmd,kdr->kmr", stash_rows, down, preferred_element_type=F32)
    back_codes = (back_codes * scale).astype(BF16)
    code_grads = jnp.einsum("kmd,krd->kmr", grad_rows, up, preferred_element_type=F32)
    code_grads = (code_grads * scale).astype(BF16)
    returned = jnp.einsum("kmr,kdr->kmd", code_grads, down, preferred_element_type=F32).astype(BF16)
    returned = returned.reshape(rows, CHIPS, CORES, BLOCK).transpose(2, 1, 0, 3)
    own_returned = lax.dynamic_index_in_dim(returned, core, axis=0, keepdims=False)
    other_returned = send(lax.dynamic_index_in_dim(returned, 1 - core, axis=0, keepdims=False), OTHER_CORE)
    returned = jnp.concatenate([own_returned, other_returned], axis=1)

    spread = (token_ids[:, None] == of_chip(bwd_token)[None, :]).astype(BF16)

    def block_at(second, first):
        z = jnp.where(core == 0, chip_z + second, chip_z + first) % SIDE
        x = jnp.where(core == 0, chip_x + first, chip_x + second) % SIDE
        return z * SIDE + x

    def partial_sums(second, firsts, received=(), takes=()):
        order = jnp.stack([block_at(second, first) for first in firsts] + [core]).astype(jnp.int32)
        grads = (cotangent, other_cotangent)
        return backward_product(order, grads, weight, other_weight, spread, returned, received, takes)

    firsts = (2, 1, 3, 0)
    far_up = send(partial_sums(2, firsts[:2]), SECOND_UP)
    far_down = send(partial_sums(2, firsts[2:]), SECOND_DOWN)
    near_up = send(partial_sums(1, firsts, (far_up,), ((0, 2),)), SECOND_UP)
    near_down = send(partial_sums(3, firsts, (far_down,), ((2, 4),)), SECOND_DOWN)
    sums = partial_sums(0, firsts, (near_up, near_down), ((0, 4), (0, 4)))
    far_up = send(sums[0, :half], FIRST_UP)
    far_down = send(sums[0, half:], FIRST_DOWN)
    near_up = jnp.concatenate([add_rounded(sums[1, :half], far_up), sums[1, half:]])
    near_down = jnp.concatenate([sums[2, :half], add_rounded(sums[2, half:], far_down)])
    near_up = send(near_up, FIRST_UP)
    near_down = send(near_down, FIRST_DOWN)
    back_out = add_rounded(cotangent, sums[3], near_up, near_down)
    next_bwd = shifted(back_out, "section", -1)[None]

    fwd_rows = (of_chip(fwd_token)[:, None] == token_ids[None, :]).astype(BF16)
    core_index = core.astype(jnp.int32).reshape(1)
    own_out, for_other_out, fwd_windows = forward_product(core_index, gathered, weight, other_weight, fwd_rows)
    other_out = send(for_other_out, OTHER_CORE)
    other_windows = send(fwd_windows[:, rows:], OTHER_CORE)
    own_windows = fwd_windows[:, :rows]
    low = jnp.where(core == 0, own_windows, other_windows)
    high = jnp.where(core == 0, other_windows, own_windows)
    fwd_windows = jnp.stack([low, high], axis=1).reshape(devices, owned, window, BLOCK)
    fwd_windows = fwd_windows.transpose(1, 2, 0, 3).reshape(owned, window, devices * BLOCK)
    codes = jnp.einsum("kmd,kdr->kmr", fwd_windows, down, preferred_element_type=F32)
    codes = (codes * scale).astype(BF16)
    adapter_out = jnp.einsum("kmr,krd->kmd", codes, up, preferred_element_type=F32).astype(BF16)
    adapter_out = adapter_out.reshape(rows, devices, BLOCK).transpose(1, 0, 2)
    adapter_out = lax.all_to_all(adapter_out, "tp", split_axis=0, concat_axis=0, tiled=True)
    put = (token_ids[:, None] == fwd_token[None, :]).astype(BF16)
    adapter_rows = jnp.dot(put, adapter_out.reshape(devices * rows, BLOCK), preferred_element_type=F32)
    layer_out = (layer_in.astype(F32) + (own_out + other_out) + adapter_rows).astype(BF16)
    next_fwd = shifted(layer_out, "section", 1)[None]

    grad_up = jnp.einsum("kmr,kmd->krd", back_codes, grad_rows, preferred_element_type=F32).astype(BF16)
    grad_down = jnp.einsum("kmd,kmr->kdr", stash_rows, code_grads, preferred_element_type=F32).astype(BF16)
    return (next_fwd, next_bwd, grad_down[None], grad_up[None])


def solution(mesh):
    placed = (
        P("section", None, "tp"),
        P("section", None, "tp"),
        P("section", None, "tp"),
        P("section", None, "tp"),
        P("section", "tp", None, None),
        P("section", "tp", None, None),
        P("section", None),
        P("section", None),
        P(),
        P(),
    )
    return jax.shard_map(
        shards,
        mesh=mesh,
        in_specs=placed,
        out_specs=(
            P("section", None, "tp"),
            P("section", None, "tp"),
            P("section", "tp", None, None),
            P("section", "tp", None, None),
        ),
        check_vma=False,
    )
```

```python
import functools
import math

import jax
import jax.numpy as jnp
from jax import lax
from jax.experimental import pallas as pl
from jax.experimental.pallas import tpu as pltpu
from jax.sharding import PartitionSpec as P

BF16 = jnp.bfloat16
F32 = jnp.float32
SIDE = 4
CHIPS = 16
CORES = 2
BLOCK = 256
SUBLANES = 8
VMEM = 16 * 1024 * 1024


def place(z, x, core):
    return (z * SIDE + x) * CORES + core


def ring_pairs(first, step):
    pairs = []
    for z in range(SIDE):
        for x in range(SIDE):
            for core in range(CORES):
                along_x = (core == 0) == first
                target = place(z, (x + step) % SIDE, core) if along_x else place((z + step) % SIDE, x, core)
                pairs.append((place(z, x, core), target))
    return pairs


FIRST_UP, FIRST_DOWN = ring_pairs(True, 1), ring_pairs(True, -1)
SECOND_UP, SECOND_DOWN = ring_pairs(False, 1), ring_pairs(False, -1)
OTHER_CORE = [(index, index ^ 1) for index in range(CHIPS * CORES)]


def send(value, pairs):
    return lax.ppermute(value, "tp", pairs)


def shifted(value, axis, steps):
    count = lax.axis_size(axis)
    pairs = [(source, (source + steps) % count) for source in range(count)]
    return lax.ppermute(value, axis, pairs)


def whole(shape):
    return pl.BlockSpec(shape, lambda *_: (0,) * len(shape))


def kernel(body, name, grid, prefetched, in_specs, outs, flops, scratch=()):
    out_shape = [jax.ShapeDtypeStruct(shape, dtype) for _, shape, dtype in outs]
    size = sum(2 * math.prod(shape) for _, shape, _ in outs)
    return pl.pallas_call(
        body,
        grid_spec=pltpu.PrefetchScalarGridSpec(
            num_scalar_prefetch=prefetched,
            grid=grid,
            in_specs=in_specs,
            out_specs=[spec for spec, _, _ in outs],
            scratch_shapes=list(scratch),
        ),
        out_shape=out_shape,
        compiler_params=pltpu.CompilerParams(vmem_limit_bytes=VMEM),
        cost_estimate=pl.CostEstimate(flops=flops, bytes_accessed=2 * size, transcendentals=0),
        name=name,
    )


def slots_body(fwd_ref, bwd_ref, ranks_ref, slot_ref, info_ref):
    adapters = slot_ref.shape[0]

    def step(adapter, starts):
        slot = slot_ref[adapter]
        fwd, bwd = fwd_ref[adapter], bwd_ref[adapter]
        for row, value in enumerate((starts[0], fwd, starts[1], bwd, ranks_ref[adapter])):
            info_ref[row * adapters + slot] = value
        return starts[0] + fwd, starts[1] + bwd

    zero = jnp.int32(0)
    lax.fori_loop(0, adapters, step, (zero, zero))


def slots(forward_counts, backward_counts, ranks, adapter_slot):
    adapters = adapter_slot.shape[0]
    scalars = pl.BlockSpec(memory_space=pltpu.SMEM)
    return pl.pallas_call(
        slots_body,
        in_specs=[scalars] * 4,
        out_specs=scalars,
        out_shape=jax.ShapeDtypeStruct((5 * adapters,), jnp.int32),
        name="slots",
    )(forward_counts[0], backward_counts[0], ranks, adapter_slot)


def slot_rows(ref, start, length, window):
    past = lax.rem(start, SUBLANES)
    size = window + SUBLANES
    rows = ref[pl.ds(pl.multiple_of(start - past, SUBLANES), size), :]
    rows = pltpu.roll(rows, lax.rem(size - past, size), 0)[:window]
    held = lax.broadcasted_iota(jnp.int32, rows.shape, 0) < length
    return jnp.where(held, rows, 0.0).astype(BF16)


def windows_body(adapters, window, each, info_ref, stash_ref, cotangent_ref, out_ref, wide_ref):
    tokens = stash_ref.shape[0]
    step = pl.program_id(0)
    owned = out_ref.shape[1] // window

    @pl.when(step == 0)
    def _():
        wide_ref[:tokens, :BLOCK] = stash_ref[...].astype(F32)
        wide_ref[:tokens, BLOCK:] = cotangent_ref[...].astype(F32)

    for index in range(each):
        slot = step * each + index
        rows = slot_rows(wide_ref, info_ref[2 * adapters + slot], info_ref[3 * adapters + slot], window)
        low = index % owned * window
        out_ref[index // owned, low : low + window] = rows


def windows_of(info, stash, cotangent, adapters, window, rows):
    devices = adapters * window // rows
    tokens = stash.shape[0]
    each = 16
    owners = each * window // rows
    out = pl.BlockSpec((owners, rows, 2 * BLOCK), lambda i, info: (i, 0, 0))
    return kernel(
        functools.partial(windows_body, adapters, window, each),
        "windows",
        (adapters // each,),
        1,
        [whole(stash.shape), whole(cotangent.shape)],
        [(out, (devices, rows, 2 * BLOCK), BF16)],
        2 * 10**9,
        [pltpu.VMEM((tokens + window + SUBLANES, 2 * BLOCK), F32)],
    )(info, stash, cotangent)[0]


NT = (((1,), (1,)), ((), ()))
TN = (((0,), (0,)), ((), ()))
GROUP = 8


def lanes(ref, *index):
    return jnp.concatenate([ref[(slot,) + index] for slot in range(ref.shape[0])], axis=1)


def codes_body(windows_ref, down_ref, up_ref, scale_ref, codes_ref, grads_ref, code_sum, grad_sum):
    step = pl.program_id(0)

    @pl.when(step == 0)
    def _():
        code_sum[...] = jnp.zeros_like(code_sum)
        grad_sum[...] = jnp.zeros_like(grad_sum)

    stash = jnp.concatenate([windows_ref[s, :, :BLOCK] for s in range(GROUP)], axis=1)
    grad = jnp.concatenate([windows_ref[s, :, BLOCK:] for s in range(GROUP)], axis=1)
    up = up_ref[...].reshape(-1, up_ref.shape[2])
    code_sum[...] += jnp.dot(stash, lanes(down_ref), preferred_element_type=F32)
    grad_sum[...] += lax.dot_general(grad, up, NT, preferred_element_type=F32)

    @pl.when(step == pl.num_programs(0) - 1)
    def _():
        codes_ref[...] = (code_sum[...] * scale_ref[...]).astype(BF16)
        grads_ref[...] = (grad_sum[...] * scale_ref[...]).astype(BF16)


def codes_of(windows, down, up, scale):
    devices, rows, _ = windows.shape
    owned, _, rank = down.shape
    shape = scale.shape
    return kernel(
        codes_body,
        "codes",
        (devices // GROUP,),
        0,
        [
            pl.BlockSpec((GROUP, rows, 2 * BLOCK), lambda i: (i, 0, 0)),
            pl.BlockSpec((owned, GROUP * BLOCK, rank), lambda i: (0, i, 0)),
            pl.BlockSpec((owned, rank, GROUP * BLOCK), lambda i: (0, 0, i)),
            whole(shape),
        ],
        [(whole(shape), shape, BF16)] * 2,
        2 * 10**9,
        [pltpu.VMEM(shape, F32)] * 2,
    )(windows, down, up, scale)


def halves(down):
    owned, _, rank = down.shape
    view = down.reshape(owned, CHIPS, CORES, BLOCK, rank)
    shape = (owned, GROUP, 1, BLOCK, rank)
    own = pl.BlockSpec(shape, lambda i, core: (0, i, core[0], 0, 0))
    other = pl.BlockSpec(shape, lambda i, core: (0, i, 1 - core[0], 0, 0))
    return view, own, other


def returned_body(core_ref, grads_ref, own_down_ref, other_down_ref, own_ref, other_ref):
    grads = grads_ref[...]
    for down_ref, out_ref in ((other_down_ref, other_ref), (own_down_ref, own_ref)):
        for index in range(GROUP):
            part = lax.dot_general(grads, lanes(down_ref, index, 0), NT, preferred_element_type=F32)
            out_ref[index] = part.astype(BF16)


def returned_of(core, code_grads, down):
    rows = code_grads.shape[0]
    view, own, other = halves(down)
    out = pl.BlockSpec((GROUP, rows, BLOCK), lambda i, core: (i, 0, 0))
    return kernel(
        returned_body,
        "returned",
        (CHIPS // GROUP,),
        1,
        [whole(code_grads.shape), own, other],
        [(out, (CHIPS, rows, BLOCK), BF16)] * 2,
        10**9,
    )(core, code_grads, view, view)


def forward_codes_body(core_ref, own_x_ref, other_x_ref, own_down_ref, other_down_ref, scale_ref, codes_ref, code_sum):
    step = pl.program_id(0)

    @pl.when(step == 0)
    def _():
        code_sum[...] = jnp.zeros_like(code_sum)

    for x_ref, down_ref in ((own_x_ref, own_down_ref), (other_x_ref, other_down_ref)):
        x = jnp.concatenate([x_ref[s] for s in range(GROUP)], axis=1)
        matrix = jnp.concatenate([lanes(down_ref, s, 0) for s in range(GROUP)], axis=0)
        code_sum[...] += jnp.dot(x, matrix, preferred_element_type=F32)

    @pl.when(step == pl.num_programs(0) - 1)
    def _():
        codes_ref[...] = (code_sum[...] * scale_ref[...]).astype(BF16)


def forward_codes_of(core, own_windows, other_windows, down, scale):
    rows = own_windows.shape[1]
    view, own, other = halves(down)
    x = pl.BlockSpec((GROUP, rows, BLOCK), lambda i, core: (i, 0, 0))
    shape = scale.shape
    return kernel(
        forward_codes_body,
        "forward_codes",
        (CHIPS // GROUP,),
        1,
        [x, x, own, other, whole(shape)],
        [(whole(shape), shape, BF16)],
        10**9,
        [pltpu.VMEM(shape, F32)],
    )(core, own_windows, other_windows, view, view, scale)[0]


def adapter_body(codes_ref, up_ref, out_ref):
    up = up_ref[...].reshape(-1, up_ref.shape[2])
    part = jnp.dot(codes_ref[...], up, preferred_element_type=F32).astype(BF16)
    for index in range(out_ref.shape[0]):
        out_ref[index] = part[:, index * BLOCK : (index + 1) * BLOCK]


def adapter_rows_of(codes, up, devices):
    rows = codes.shape[0]
    owned, rank, _ = up.shape
    group = GROUP
    out = pl.BlockSpec((group, rows, BLOCK), lambda i: (i, 0, 0))
    return kernel(
        adapter_body,
        "adapter_rows",
        (devices // group,),
        0,
        [whole(codes.shape), pl.BlockSpec((owned, rank, group * BLOCK), lambda i: (0, 0, i))],
        [(out, (devices, rows, BLOCK), BF16)],
        10**9,
    )(codes, up)[0]


def gradients_body(windows_ref, codes_ref, grads_ref, down_ref, up_ref):
    owned, _, rank = down_ref.shape
    for s in range(GROUP):
        span = slice(s * BLOCK, (s + 1) * BLOCK)
        stash, grad = windows_ref[s, :, :BLOCK], windows_ref[s, :, BLOCK:]
        down = lax.dot_general(stash, grads_ref[...], TN, preferred_element_type=F32).astype(BF16)
        up = lax.dot_general(codes_ref[...], grad, TN, preferred_element_type=F32).astype(BF16)
        for slot in range(owned):
            own = slice(slot * rank, (slot + 1) * rank)
            down_ref[slot, span] = down[:, own]
            up_ref[slot, :, span] = up[own]


def gradients_of(windows, back_codes, code_grads, owned):
    devices, rows, _ = windows.shape
    rank = back_codes.shape[1] // owned
    width = devices * BLOCK
    return kernel(
        gradients_body,
        "gradients",
        (devices // GROUP,),
        0,
        [
            pl.BlockSpec((GROUP, rows, 2 * BLOCK), lambda i: (i, 0, 0)),
            whole(back_codes.shape),
            whole(code_grads.shape),
        ],
        [
            (pl.BlockSpec((owned, GROUP * BLOCK, rank), lambda i: (0, i, 0)), (owned, width, rank), BF16),
            (pl.BlockSpec((owned, rank, GROUP * BLOCK), lambda i: (0, 0, i)), (owned, rank, width), BF16),
        ],
        2 * 10**9,
    )(windows, back_codes, code_grads)


PAIR = 2


def forward_body(window, order_ref, info_ref, *rest):
    pieces, rest = rest[:13], rest[13:]
    own_w, other_w, rest = rest[:PAIR], rest[PAIR : 2 * PAIR], rest[2 * PAIR :]
    own_ref, other_ref, own_x_ref, other_x_ref, wide_ref = rest
    step = pl.program_id(0)
    tokens = own_ref.shape[0]
    core = order_ref[CHIPS]
    chip = order_ref[CHIPS + 1]
    adapters = info_ref.shape[0] // 5
    owned = own_x_ref.shape[1] // window

    @pl.when(step == 0)
    def _():
        own_ref[...] = jnp.zeros_like(own_ref)
        other_ref[...] = jnp.zeros_like(other_ref)

    def take(*blocks):
        own_sum, other_sum = own_ref[...], other_ref[...]
        for index, (x_ref, at) in enumerate(blocks):
            x = x_ref[...] if at is None else x_ref[at]
            own_sum += jnp.dot(x, own_w[index][0, 0], preferred_element_type=F32)
            other_sum += jnp.dot(x, other_w[index][0], preferred_element_type=F32)
            wide_ref[:tokens] = x.astype(F32)
            at = order_ref[PAIR * step + index]
            for whose, out_ref in ((core, own_x_ref), (1 - core, other_x_ref)):
                for slot in range(owned):
                    place_of = (chip * CORES + whose) * owned + slot
                    rows = slot_rows(wide_ref, info_ref[place_of], info_ref[adapters + place_of], window)
                    out_ref[at, slot * window : (slot + 1) * window] = rows
        own_ref[...] = own_sum
        other_ref[...] = other_sum

    own, far, near = pieces[0:9:3], pieces[1:9:3], pieces[2:9:3]
    pairs = []
    for line in range(3):
        pairs += [((own[line], None), (far[line], None)), ((near[line], 0), (near[line], 1))]
    pairs += [((pieces[9], None), (pieces[10], None)), ((pieces[11], None), (pieces[12], None))]
    for index, pair in enumerate(pairs):
        pl.when(step == index)(functools.partial(take, *pair))


def forward_product(order, info, pieces, weight, other_weight, window, rows):
    tokens = pieces[0].shape[0]
    product = (whole((tokens, BLOCK)), (tokens, BLOCK), F32)
    windows = (whole((CHIPS, rows, BLOCK)), (CHIPS, rows, BLOCK), BF16)

    def own(index):
        shape = (1, 1, BLOCK, BLOCK)
        return pl.BlockSpec(shape, lambda k, order, info: (order[PAIR * k + index], order[CHIPS], 0, 0))

    def other(index):
        return pl.BlockSpec((1, BLOCK, BLOCK), lambda k, order, info: (order[PAIR * k + index], 0, 0))

    return kernel(
        functools.partial(forward_body, window),
        "forward_product",
        (CHIPS // PAIR,),
        2,
        [whole(piece.shape) for piece in pieces]
        + [own(index) for index in range(PAIR)]
        + [other(index) for index in range(PAIR)],
        [product, product, windows, windows],
        9 * 10**9,
        [pltpu.VMEM((tokens + window + SUBLANES, BLOCK), F32)],
    )(order, info, *pieces, *[weight] * PAIR, *[other_weight] * PAIR)


def backward_body(takes, order_ref, grad_ref, own_w_ref, other_w_ref, spread_ref, own_ret_ref, other_ret_ref, *rest):
    received, out_ref = rest[:-1], rest[-1]
    step = pl.program_id(0)
    matrix = jnp.concatenate([own_w_ref[0, 0], other_w_ref[0]], axis=1)
    returned = jnp.concatenate([own_ret_ref[0], other_ret_ref[0]], axis=0)
    tile = 2 * BLOCK
    for low in range(0, grad_ref.shape[0], tile):
        span = slice(low, low + tile)
        total = lax.dot_general(grad_ref[span], matrix, NT, preferred_element_type=F32)
        total += jnp.dot(spread_ref[span], returned, preferred_element_type=F32)
        for ref, (first, last) in zip(received, takes):
            inside = (step >= first) & (step < last)
            total += jnp.where(inside, ref[0, span].astype(F32), 0.0)
        out_ref[0, span] = total.astype(BF16)


def backward_product(order, base, blocks, grads, weight, other_weight, spread, returned, received=(), takes=()):
    tokens = grads.shape[0]
    core_at = CHIPS

    def taken(bounds):
        first, last = bounds
        return pl.BlockSpec((1, tokens, BLOCK), lambda j, order: (jnp.clip(j - first, 0, last - first - 1), 0, 0))

    rows = pl.BlockSpec((1,) + returned[0].shape[1:], lambda j, order: (order[base + j], 0, 0))
    out = pl.BlockSpec((1, tokens, BLOCK), lambda j, order: (j, 0, 0))
    return kernel(
        functools.partial(backward_body, takes),
        "backward_product",
        (blocks,),
        1,
        [
            whole(grads.shape),
            pl.BlockSpec((1, 1, BLOCK, BLOCK), lambda j, order: (order[base + j], order[core_at], 0, 0)),
            pl.BlockSpec((1, BLOCK, BLOCK), lambda j, order: (order[base + j], 0, 0)),
            whole(spread.shape),
            rows,
            rows,
        ]
        + [taken(bounds) for bounds in takes],
        [(out, (blocks, tokens, BLOCK), BF16)],
        blocks * 34 * 10**7,
    )(order, grads, weight, other_weight, spread, *returned, *received)[0]


def add_rounded(*values):
    total = values[0].astype(F32)
    for value in values[1:]:
        total = total + value.astype(F32)
    return total.astype(BF16)


def shards(
    forward_inputs,
    backward_inputs,
    backward_cotangents,
    frozen_weight,
    adapter_down_weight,
    adapter_up_weight,
    forward_counts,
    backward_counts,
    ranks,
    adapter_slot,
):
    tokens = forward_inputs.shape[1]
    adapters = adapter_slot.shape[0]
    owned = adapter_down_weight.shape[1]
    rank = adapter_down_weight.shape[3]
    window = 2 * tokens // adapters
    rows = owned * window
    devices = CHIPS * CORES
    half = tokens // 2
    device = lax.axis_index("tp")
    core = device % CORES
    chip = device // CORES
    chip_z, chip_x = chip // SIDE, chip % SIDE

    layer_in = forward_inputs[0]
    stash = backward_inputs[0]
    cotangent = backward_cotangents[0]
    weight = frozen_weight[0].reshape(CHIPS, CORES, BLOCK, BLOCK)
    down = adapter_down_weight[0]
    up = adapter_up_weight[0]

    below, above = send(layer_in, FIRST_UP), send(layer_in, FIRST_DOWN)
    own_below, own_above = send(layer_in, SECOND_UP), send(layer_in, SECOND_DOWN)
    far_low, far_high = send(below[:half], FIRST_UP), send(above[half:], FIRST_DOWN)
    own_far = send(own_below, SECOND_UP)
    near = jnp.stack([below, above])
    near_below, near_above = send(near, SECOND_UP), send(near, SECOND_DOWN)
    far = jnp.concatenate([far_low, far_high])
    far_below, far_above = send(far, SECOND_UP), send(far, SECOND_DOWN)
    below_far, above_far = send(near_below[0], SECOND_UP), send(near_above[1], SECOND_DOWN)
    far_far = send(far_above, SECOND_DOWN)
    pieces = (layer_in, far, near, own_below, far_below, near_below, own_above, far_above, near_above)
    pieces += (own_far, far_far, below_far, above_far)

    for_other = lax.dynamic_index_in_dim(weight, 1 - core, axis=1, keepdims=False)
    other_weight = send(for_other, OTHER_CORE)
    other_cotangent = send(cotangent, OTHER_CORE)

    info = slots(forward_counts, backward_counts, ranks, adapter_slot)
    windows = windows_of(info, stash, cotangent, adapters, window, rows)
    windows = lax.all_to_all(windows, "tp", split_axis=0, concat_axis=0, tiled=True)

    starts = info.reshape(5, adapters)
    offsets = jnp.arange(window, dtype=jnp.int32)
    token_ids = jnp.arange(tokens, dtype=jnp.int32)

    def tokens_of(start, length):
        token = jnp.where(offsets[None, :] < length[:, None], start[:, None] + offsets[None, :], -1)
        return token.reshape(-1)

    def of_chip(token):
        mine = lax.dynamic_slice_in_dim(token, device * rows, rows)
        other = lax.dynamic_slice_in_dim(token, (device ^ 1) * rows, rows)
        return jnp.concatenate([mine, other])

    fwd_token = tokens_of(starts[0], starts[1])
    bwd_token = tokens_of(starts[2], starts[3])
    own_rank = lax.dynamic_slice_in_dim(starts[4], device * owned, owned)
    column = jnp.arange(owned * rank, dtype=jnp.int32)
    row = jnp.arange(rows, dtype=jnp.int32)
    factor = jnp.repeat(8.0 / jnp.sqrt(own_rank.astype(F32)), rank)
    live = column % rank < jnp.repeat(own_rank, rank)
    mine = row[:, None] // window == column[None, :] // rank
    scale = jnp.where(mine & live[None, :], factor[None, :], 0.0)
    spread = (token_ids[:, None] == of_chip(bwd_token)[None, :]).astype(BF16)
    put = (token_ids[:, None] == fwd_token[None, :]).astype(BF16)
    core_index = core.astype(jnp.int32).reshape(1)

    def chips(pairs):
        second, first = (jnp.array(list(offsets), jnp.int32) for offsets in zip(*pairs))
        z = jnp.where(core == 0, chip_z + second, chip_z + first) % SIDE
        x = jnp.where(core == 0, chip_x + first, chip_x + second) % SIDE
        return jnp.concatenate([z * SIDE + x, core.reshape(1), chip.reshape(1)]).astype(jnp.int32)

    order = chips([(s, f) for s in (2, 1, 3, 0) for f in (2, 1, 3, 0)])
    arrivals = chips([(s, f) for s in (0, 3, 1, 2) for f in (0, 2, 3, 1)])
    grads = jnp.concatenate([cotangent, other_cotangent], axis=1)

    ready = (windows, scale, spread, grads, order, arrivals)
    windows, scale, spread, grads, order, arrivals = lax.optimization_barrier(ready)
    back_codes, code_grads = codes_of(windows, down, up, scale)
    own_returned, for_other = returned_of(core_index, code_grads, down)
    returned = (own_returned, send(for_other, OTHER_CORE))

    def partial_sums(base, blocks, received=(), takes=(), grads=grads):
        return backward_product(order, base, blocks, grads, weight, other_weight, spread, returned, received, takes)

    far_up = send(partial_sums(0, 2), SECOND_UP)
    far_down = send(partial_sums(2, 2), SECOND_DOWN)
    own_out, for_other_out, own_x, for_other_x = forward_product(
        arrivals, info, pieces, weight, other_weight, window, rows
    )
    other_x = send(for_other_x, OTHER_CORE)
    other_out = send(for_other_out, OTHER_CORE)

    later_grads, _ = lax.optimization_barrier((grads, own_out))
    near_up = send(partial_sums(4, 4, (far_up,), ((0, 2),), later_grads), SECOND_UP)
    near_down = send(partial_sums(8, 4, (far_down,), ((2, 4),), later_grads), SECOND_DOWN)

    codes = forward_codes_of(core_index, own_x, other_x, down, scale)
    adapter_out = adapter_rows_of(codes, up, devices)
    later_grads, _ = lax.optimization_barrier((grads, adapter_out))
    sums = partial_sums(12, 4, (near_up, near_down), ((0, 4), (0, 4)), later_grads)
    far_up = send(sums[0, :half], FIRST_UP)
    far_down = send(sums[0, half:], FIRST_DOWN)
    near_up = jnp.concatenate([add_rounded(sums[1, :half], far_up), sums[1, half:]])
    near_down = jnp.concatenate([sums[2, :half], add_rounded(sums[2, half:], far_down)])
    near_up = send(near_up, FIRST_UP)
    near_down = send(near_down, FIRST_DOWN)
    back_out = add_rounded(cotangent, sums[3], near_up, near_down)
    next_bwd = shifted(back_out, "section", -1)[None]

    adapter_out = lax.all_to_all(adapter_out, "tp", split_axis=0, concat_axis=0, tiled=True)
    adapter_rows = jnp.dot(put, adapter_out.reshape(devices * rows, BLOCK), preferred_element_type=F32)
    layer_out = (layer_in.astype(F32) + (own_out + other_out) + adapter_rows).astype(BF16)
    next_fwd = shifted(layer_out, "section", 1)[None]

    grad_down, grad_up = gradients_of(windows, back_codes, code_grads, owned)
    return (next_fwd, next_bwd, grad_down[None], grad_up[None])


def solution(mesh):
    placed = (
        P("section", None, "tp"),
        P("section", None, "tp"),
        P("section", None, "tp"),
        P("section", None, "tp"),
        P("section", "tp", None, None),
        P("section", "tp", None, None),
        P("section", None),
        P("section", None),
        P(),
        P(),
    )
    return jax.shard_map(
        shards,
        mesh=mesh,
        in_specs=placed,
        out_specs=(
            P("section", None, "tp"),
            P("section", None, "tp"),
            P("section", "tp", None, None),
            P("section", "tp", None, None),
        ),
        check_vma=False,
    )
```

```python
import functools
import math

import jax
import jax.numpy as jnp
from jax import lax
from jax.experimental import pallas as pl
from jax.experimental.pallas import tpu as pltpu
from jax.sharding import PartitionSpec as P

BF16 = jnp.bfloat16
F32 = jnp.float32
SIDE = 4
CHIPS = 16
CORES = 2
BLOCK = 256
SUBLANES = 8
VMEM = 16 * 1024 * 1024


def place(z, x, core):
    return (z * SIDE + x) * CORES + core


def ring_pairs(first, step):
    pairs = []
    for z in range(SIDE):
        for x in range(SIDE):
            for core in range(CORES):
                along_x = (core == 0) == first
                target = place(z, (x + step) % SIDE, core) if along_x else place((z + step) % SIDE, x, core)
                pairs.append((place(z, x, core), target))
    return pairs


FIRST_UP, FIRST_DOWN = ring_pairs(True, 1), ring_pairs(True, -1)
SECOND_UP, SECOND_DOWN = ring_pairs(False, 1), ring_pairs(False, -1)
OTHER_CORE = [(index, index ^ 1) for index in range(CHIPS * CORES)]


def send(value, pairs):
    return lax.ppermute(value, "tp", pairs)


def shifted(value, axis, steps):
    count = lax.axis_size(axis)
    pairs = [(source, (source + steps) % count) for source in range(count)]
    return lax.ppermute(value, axis, pairs)


def whole(shape):
    return pl.BlockSpec(shape, lambda *_: (0,) * len(shape))


def kernel(body, name, grid, prefetched, in_specs, outs, flops, scratch=()):
    out_shape = [jax.ShapeDtypeStruct(shape, dtype) for _, shape, dtype in outs]
    size = sum(2 * math.prod(shape) for _, shape, _ in outs)
    return pl.pallas_call(
        body,
        grid_spec=pltpu.PrefetchScalarGridSpec(
            num_scalar_prefetch=prefetched,
            grid=grid,
            in_specs=in_specs,
            out_specs=[spec for spec, _, _ in outs],
            scratch_shapes=list(scratch),
        ),
        out_shape=out_shape,
        compiler_params=pltpu.CompilerParams(vmem_limit_bytes=VMEM),
        cost_estimate=pl.CostEstimate(flops=flops, bytes_accessed=2 * size, transcendentals=0),
        name=name,
    )


def slots_body(fwd_ref, bwd_ref, ranks_ref, slot_ref, info_ref):
    adapters = slot_ref.shape[0]

    def step(adapter, starts):
        slot = slot_ref[adapter]
        fwd, bwd = fwd_ref[adapter], bwd_ref[adapter]
        for row, value in enumerate((starts[0], fwd, starts[1], bwd, ranks_ref[adapter])):
            info_ref[row * adapters + slot] = value
        return starts[0] + fwd, starts[1] + bwd

    zero = jnp.int32(0)
    lax.fori_loop(0, adapters, step, (zero, zero))


def slots(forward_counts, backward_counts, ranks, adapter_slot):
    adapters = adapter_slot.shape[0]
    scalars = pl.BlockSpec(memory_space=pltpu.SMEM)
    return pl.pallas_call(
        slots_body,
        in_specs=[scalars] * 4,
        out_specs=scalars,
        out_shape=jax.ShapeDtypeStruct((5 * adapters,), jnp.int32),
        name="slots",
    )(forward_counts[0], backward_counts[0], ranks, adapter_slot)


def slot_rows(ref, start, length, window):
    past = lax.rem(start, SUBLANES)
    size = window + SUBLANES
    rows = ref[pl.ds(pl.multiple_of(start - past, SUBLANES), size), :]
    rows = pltpu.roll(rows, lax.rem(size - past, size), 0)[:window]
    held = lax.broadcasted_iota(jnp.int32, rows.shape, 0) < length
    return jnp.where(held, rows, 0.0).astype(BF16)


def windows_body(adapters, window, each, info_ref, stash_ref, cotangent_ref, stash_out_ref, cotangent_out_ref, wide_ref):
    tokens = stash_ref.shape[0]
    step = pl.program_id(0)
    owned = stash_out_ref.shape[1] // window

    @pl.when(step == 0)
    def _():
        wide_ref[:tokens, :BLOCK] = stash_ref[...].astype(F32)
        wide_ref[:tokens, BLOCK:] = cotangent_ref[...].astype(F32)

    for index in range(each):
        slot = step * each + index
        rows = slot_rows(wide_ref, info_ref[2 * adapters + slot], info_ref[3 * adapters + slot], window)
        low = index % owned * window
        stash_out_ref[index // owned, low : low + window] = rows[:, :BLOCK]
        cotangent_out_ref[index // owned, low : low + window] = rows[:, BLOCK:]


def windows_of(info, stash, cotangent, adapters, window, rows):
    devices = adapters * window // rows
    tokens = stash.shape[0]
    each = 16
    owners = each * window // rows
    out = pl.BlockSpec((owners, rows, BLOCK), lambda i, info: (i, 0, 0))
    return kernel(
        functools.partial(windows_body, adapters, window, each),
        "windows",
        (adapters // each,),
        1,
        [whole(stash.shape), whole(cotangent.shape)],
        [(out, (devices, rows, BLOCK), BF16)] * 2,
        2 * 10**9,
        [pltpu.VMEM((tokens + window + SUBLANES, 2 * BLOCK), F32)],
    )(info, stash, cotangent)


NT = (((1,), (1,)), ((), ()))
TN = (((0,), (0,)), ((), ()))
GROUP = 8


def lanes(ref, *index):
    return jnp.concatenate([ref[(slot,) + index] for slot in range(ref.shape[0])], axis=1)


def code_grads_body(windows_ref, up_ref, scale_ref, grads_ref, grad_sum):
    step = pl.program_id(0)

    @pl.when(step == 0)
    def _():
        grad_sum[...] = jnp.zeros_like(grad_sum)

    grad = jnp.concatenate([windows_ref[s] for s in range(GROUP)], axis=1)
    up = up_ref[...].reshape(-1, up_ref.shape[2])
    grad_sum[...] += lax.dot_general(grad, up, NT, preferred_element_type=F32)

    @pl.when(step == pl.num_programs(0) - 1)
    def _():
        grads_ref[...] = (grad_sum[...] * scale_ref[...]).astype(BF16)


def code_grads_of(windows, up, scale):
    devices, rows, _ = windows.shape
    owned, rank, _ = up.shape
    shape = scale.shape
    return kernel(
        code_grads_body,
        "code_grads",
        (devices // GROUP,),
        0,
        [
            pl.BlockSpec((GROUP, rows, BLOCK), lambda i: (i, 0, 0)),
            pl.BlockSpec((owned, rank, GROUP * BLOCK), lambda i: (0, 0, i)),
            whole(shape),
        ],
        [(whole(shape), shape, BF16)],
        10**9,
        [pltpu.VMEM(shape, F32)],
    )(windows, up, scale)[0]


def back_codes_body(windows_ref, down_ref, scale_ref, codes_ref, code_sum):
    step = pl.program_id(0)

    @pl.when(step == 0)
    def _():
        code_sum[...] = jnp.zeros_like(code_sum)

    stash = jnp.concatenate([windows_ref[s] for s in range(GROUP)], axis=1)
    code_sum[...] += jnp.dot(stash, lanes(down_ref), preferred_element_type=F32)

    @pl.when(step == pl.num_programs(0) - 1)
    def _():
        codes_ref[...] = (code_sum[...] * scale_ref[...]).astype(BF16)


def back_codes_of(windows, down, scale):
    devices, rows, _ = windows.shape
    owned, _, rank = down.shape
    shape = scale.shape
    return kernel(
        back_codes_body,
        "back_codes",
        (devices // GROUP,),
        0,
        [
            pl.BlockSpec((GROUP, rows, BLOCK), lambda i: (i, 0, 0)),
            pl.BlockSpec((owned, GROUP * BLOCK, rank), lambda i: (0, i, 0)),
            whole(shape),
        ],
        [(whole(shape), shape, BF16)],
        10**9,
        [pltpu.VMEM(shape, F32)],
    )(windows, down, scale)[0]


def halves(down):
    owned, _, rank = down.shape
    view = down.reshape(owned, CHIPS, CORES, BLOCK, rank)
    shape = (owned, GROUP, 1, BLOCK, rank)
    own = pl.BlockSpec(shape, lambda i, core: (0, i, core[0], 0, 0))
    other = pl.BlockSpec(shape, lambda i, core: (0, i, 1 - core[0], 0, 0))
    return view, own, other


def returned_body(core_ref, grads_ref, own_down_ref, other_down_ref, own_ref, other_ref):
    grads = grads_ref[...]
    for down_ref, out_ref in ((other_down_ref, other_ref), (own_down_ref, own_ref)):
        for index in range(GROUP):
            part = lax.dot_general(grads, lanes(down_ref, index, 0), NT, preferred_element_type=F32)
            out_ref[index] = part.astype(BF16)


def returned_of(core, code_grads, down):
    rows = code_grads.shape[0]
    view, own, other = halves(down)
    out = pl.BlockSpec((GROUP, rows, BLOCK), lambda i, core: (i, 0, 0))
    return kernel(
        returned_body,
        "returned",
        (CHIPS // GROUP,),
        1,
        [whole(code_grads.shape), own, other],
        [(out, (CHIPS, rows, BLOCK), BF16)] * 2,
        10**9,
    )(core, code_grads, view, view)


def forward_codes_body(core_ref, own_x_ref, other_x_ref, own_down_ref, other_down_ref, scale_ref, codes_ref, code_sum):
    step = pl.program_id(0)

    @pl.when(step == 0)
    def _():
        code_sum[...] = jnp.zeros_like(code_sum)

    for x_ref, down_ref in ((own_x_ref, own_down_ref), (other_x_ref, other_down_ref)):
        x = jnp.concatenate([x_ref[s] for s in range(GROUP)], axis=1)
        matrix = jnp.concatenate([lanes(down_ref, s, 0) for s in range(GROUP)], axis=0)
        code_sum[...] += jnp.dot(x, matrix, preferred_element_type=F32)

    @pl.when(step == pl.num_programs(0) - 1)
    def _():
        codes_ref[...] = (code_sum[...] * scale_ref[...]).astype(BF16)


def forward_codes_of(core, own_windows, other_windows, down, scale):
    rows = own_windows.shape[1]
    view, own, other = halves(down)
    x = pl.BlockSpec((GROUP, rows, BLOCK), lambda i, core: (i, 0, 0))
    shape = scale.shape
    return kernel(
        forward_codes_body,
        "forward_codes",
        (CHIPS // GROUP,),
        1,
        [x, x, own, other, whole(shape)],
        [(whole(shape), shape, BF16)],
        10**9,
        [pltpu.VMEM(shape, F32)],
    )(core, own_windows, other_windows, view, view, scale)[0]


def adapter_body(codes_ref, up_ref, out_ref):
    up = up_ref[...].reshape(-1, up_ref.shape[2])
    part = jnp.dot(codes_ref[...], up, preferred_element_type=F32).astype(BF16)
    for index in range(out_ref.shape[0]):
        out_ref[index] = part[:, index * BLOCK : (index + 1) * BLOCK]


def adapter_rows_of(codes, up, devices):
    rows = codes.shape[0]
    owned, rank, _ = up.shape
    out = pl.BlockSpec((GROUP, rows, BLOCK), lambda i: (i, 0, 0))
    return kernel(
        adapter_body,
        "adapter_rows",
        (devices // GROUP,),
        0,
        [whole(codes.shape), pl.BlockSpec((owned, rank, GROUP * BLOCK), lambda i: (0, 0, i))],
        [(out, (devices, rows, BLOCK), BF16)],
        10**9,
    )(codes, up)[0]


def forward_sum_body(window, info_ref, x_ref, own_ref, other_ref, adapter_ref, out_ref, wide_ref):
    tokens = x_ref.shape[0]
    wide_ref[:tokens] = x_ref[...].astype(F32) + (own_ref[...] + other_ref[...])
    devices, rows, _ = adapter_ref.shape
    owned = rows // window
    spare = jnp.zeros((SUBLANES, BLOCK), F32)
    for slot in range(devices * owned):
        start = info_ref[slot]
        past = lax.rem(start, SUBLANES)
        low = slot % owned * window
        added = adapter_ref[slot // owned, low : low + window].astype(F32)
        added = pltpu.roll(jnp.concatenate([added, spare]), past, 0)
        span = pl.ds(pl.multiple_of(start - past, SUBLANES), window + SUBLANES)
        wide_ref[span, :] += added
    out_ref[...] = wide_ref[:tokens].astype(BF16)


def forward_sum(info, layer_in, own_out, other_out, arrived, window):
    devices, rows, _ = arrived.shape
    shape = layer_in.shape
    adapter = pl.BlockSpec((devices, rows, BLOCK), lambda i, info: (0, 0, 0))
    return kernel(
        functools.partial(forward_sum_body, window),
        "forward_sum",
        (1,),
        1,
        [whole(shape), whole(shape), whole(shape), adapter],
        [(whole(shape), shape, BF16)],
        10**8,
        [pltpu.VMEM((shape[0] + window + SUBLANES, BLOCK), F32)],
    )(info, layer_in, own_out, other_out, arrived)[0]


def gradients_body(stash_ref, grad_ref, codes_ref, grads_ref, down_ref, up_ref):
    owned, _, rank = down_ref.shape
    for s in range(GROUP):
        span = slice(s * BLOCK, (s + 1) * BLOCK)
        down = lax.dot_general(stash_ref[s], grads_ref[...], TN, preferred_element_type=F32).astype(BF16)
        up = lax.dot_general(codes_ref[...], grad_ref[s], TN, preferred_element_type=F32).astype(BF16)
        for slot in range(owned):
            own = slice(slot * rank, (slot + 1) * rank)
            down_ref[slot, span] = down[:, own]
            up_ref[slot, :, span] = up[own]


def gradients_of(stash_windows, grad_windows, back_codes, code_grads, owned):
    devices, rows, _ = grad_windows.shape
    rank = back_codes.shape[1] // owned
    width = devices * BLOCK
    return kernel(
        gradients_body,
        "gradients",
        (devices // GROUP,),
        0,
        [
            pl.BlockSpec((GROUP, rows, BLOCK), lambda i: (i, 0, 0)),
            pl.BlockSpec((GROUP, rows, BLOCK), lambda i: (i, 0, 0)),
            whole(back_codes.shape),
            whole(code_grads.shape),
        ],
        [
            (pl.BlockSpec((owned, GROUP * BLOCK, rank), lambda i: (0, i, 0)), (owned, width, rank), BF16),
            (pl.BlockSpec((owned, rank, GROUP * BLOCK), lambda i: (0, 0, i)), (owned, rank, width), BF16),
        ],
        2 * 10**9,
    )(stash_windows, grad_windows, back_codes, code_grads)


PAIR = 2


def forward_body(window, order_ref, info_ref, *rest):
    pieces, rest = rest[:12], rest[12:]
    own_w, other_w, rest = rest[:PAIR], rest[PAIR : 2 * PAIR], rest[2 * PAIR :]
    own_ref, other_ref, own_x_ref, other_x_ref, wide_ref = rest
    step = pl.program_id(0)
    tokens = own_ref.shape[0]
    core = order_ref[CHIPS]
    chip = order_ref[CHIPS + 1]
    adapters = info_ref.shape[0] // 5
    owned = own_x_ref.shape[1] // window

    @pl.when(step == 0)
    def _():
        own_ref[...] = jnp.zeros_like(own_ref)
        other_ref[...] = jnp.zeros_like(other_ref)

    def take(*blocks):
        own_sum, other_sum = own_ref[...], other_ref[...]
        for index, (x_ref, at) in enumerate(blocks):
            x = x_ref[...] if at is None else x_ref[at]
            own_sum += jnp.dot(x, own_w[index][0, 0], preferred_element_type=F32)
            other_sum += jnp.dot(x, other_w[index][0], preferred_element_type=F32)
            wide_ref[:tokens] = x.astype(F32)
            at = order_ref[PAIR * step + index]
            for whose, out_ref in ((core, own_x_ref), (1 - core, other_x_ref)):
                for slot in range(owned):
                    place_of = (chip * CORES + whose) * owned + slot
                    rows = slot_rows(wide_ref, info_ref[place_of], info_ref[adapters + place_of], window)
                    out_ref[at, slot * window : (slot + 1) * window] = rows
        own_ref[...] = own_sum
        other_ref[...] = other_sum

    own, far, near = pieces[0::3], pieces[1::3], pieces[2::3]
    pairs = []
    for line in range(SIDE):
        pairs += [((own[line], None), (far[line], None)), ((near[line], 0), (near[line], 1))]
    for index, pair in enumerate(pairs):
        pl.when(step == index)(functools.partial(take, *pair))


def forward_product(order, info, pieces, weight, other_weight, window, rows):
    tokens = pieces[0].shape[0]
    product = (whole((tokens, BLOCK)), (tokens, BLOCK), F32)
    windows = (whole((CHIPS, rows, BLOCK)), (CHIPS, rows, BLOCK), BF16)

    def own(index):
        shape = (1, 1, BLOCK, BLOCK)
        return pl.BlockSpec(shape, lambda k, order, info: (order[PAIR * k + index], order[CHIPS], 0, 0))

    def other(index):
        return pl.BlockSpec((1, BLOCK, BLOCK), lambda k, order, info: (order[PAIR * k + index], 0, 0))

    return kernel(
        functools.partial(forward_body, window),
        "forward_product",
        (CHIPS // PAIR,),
        2,
        [whole(piece.shape) for piece in pieces]
        + [own(index) for index in range(PAIR)]
        + [other(index) for index in range(PAIR)],
        [product, product, windows, windows],
        9 * 10**9,
        [pltpu.VMEM((tokens + window + SUBLANES, BLOCK), F32)],
    )(order, info, *pieces, *[weight] * PAIR, *[other_weight] * PAIR)


def backward_body(sizes, order_ref, grad_ref, own_w_ref, other_w_ref, spread_ref, own_ret_ref, other_ret_ref, *outs):
    step = pl.program_id(0)
    matrix = jnp.concatenate([own_w_ref[0, 0], other_w_ref[0]], axis=1)
    returned = jnp.concatenate([own_ret_ref[0], other_ret_ref[0]], axis=0)
    total = lax.dot_general(grad_ref[...], matrix, NT, preferred_element_type=F32)
    total += jnp.dot(spread_ref[...], returned, preferred_element_type=F32)
    total = total.astype(BF16)
    low = 0
    for out_ref, size in zip(outs, sizes):

        @pl.when((step >= low) & (step < low + size))
        def _(out_ref=out_ref):
            out_ref[0] = total

        low += size


def backward_product(order, base, sizes, grads, weight, other_weight, spread, returned):
    tokens = grads.shape[0]
    blocks = sum(sizes)

    def out(index):
        low, size = sum(sizes[:index]), sizes[index]
        return pl.BlockSpec((1, tokens, BLOCK), lambda j, order: (jnp.clip(j - low, 0, size - 1), 0, 0))

    rows = pl.BlockSpec((1,) + returned[0].shape[1:], lambda j, order: (order[base + j], 0, 0))
    return kernel(
        functools.partial(backward_body, sizes),
        "backward_product",
        (blocks,),
        1,
        [
            whole(grads.shape),
            pl.BlockSpec((1, 1, BLOCK, BLOCK), lambda j, order: (order[base + j], order[CHIPS], 0, 0)),
            pl.BlockSpec((1, BLOCK, BLOCK), lambda j, order: (order[base + j], 0, 0)),
            whole(spread.shape),
            rows,
            rows,
        ],
        [(out(index), (size, tokens, BLOCK), BF16) for index, size in enumerate(sizes)],
        blocks * 34 * 10**7,
    )(order, grads, weight, other_weight, spread, *returned)


def total_of(*values):
    total = values[0].astype(F32)
    for value in values[1:]:
        total = total + value.astype(F32)
    return total


def add_rounded(*values):
    return total_of(*values).astype(BF16)


def shards(
    forward_inputs,
    backward_inputs,
    backward_cotangents,
    frozen_weight,
    adapter_down_weight,
    adapter_up_weight,
    forward_counts,
    backward_counts,
    ranks,
    adapter_slot,
):
    tokens = forward_inputs.shape[1]
    adapters = adapter_slot.shape[0]
    owned = adapter_down_weight.shape[1]
    rank = adapter_down_weight.shape[3]
    window = 2 * tokens // adapters
    rows = owned * window
    devices = CHIPS * CORES
    device = lax.axis_index("tp")
    core = device % CORES
    chip = device // CORES
    chip_z, chip_x = chip // SIDE, chip % SIDE

    layer_in = forward_inputs[0]
    stash = backward_inputs[0]
    cotangent = backward_cotangents[0]
    weight = frozen_weight[0].reshape(CHIPS, CORES, BLOCK, BLOCK)
    down = adapter_down_weight[0]
    up = adapter_up_weight[0]

    below, above = send(layer_in, FIRST_UP), send(layer_in, FIRST_DOWN)
    own_below, own_above = send(layer_in, SECOND_UP), send(layer_in, SECOND_DOWN)
    far = send(below, FIRST_UP)
    near = jnp.stack([below, above])
    near_below, near_above = send(near, SECOND_UP), send(near, SECOND_DOWN)
    far_below, far_above = send(far, SECOND_UP), send(far, SECOND_DOWN)
    own_far = send(own_above, SECOND_DOWN)
    near_far = send(near_below, SECOND_UP)
    far_far = send(far_above, SECOND_DOWN)
    pieces = (layer_in, far, near, own_below, far_below, near_below, own_above, far_above, near_above)
    pieces += (own_far, far_far, near_far)

    for_other = lax.dynamic_index_in_dim(weight, 1 - core, axis=1, keepdims=False)
    other_weight = send(for_other, OTHER_CORE)
    other_cotangent = send(cotangent, OTHER_CORE)

    info = slots(forward_counts, backward_counts, ranks, adapter_slot)
    stash_windows, grad_windows = windows_of(info, stash, cotangent, adapters, window, rows)
    grad_windows = lax.all_to_all(grad_windows, "tp", split_axis=0, concat_axis=0, tiled=True)

    stash_windows, other_weight = lax.optimization_barrier((stash_windows, other_weight))
    stash_windows = lax.all_to_all(stash_windows, "tp", split_axis=0, concat_axis=0, tiled=True)

    starts = info.reshape(5, adapters)
    offsets = jnp.arange(window, dtype=jnp.int32)
    token_ids = jnp.arange(tokens, dtype=jnp.int32)

    def tokens_of(start, length):
        token = jnp.where(offsets[None, :] < length[:, None], start[:, None] + offsets[None, :], -1)
        return token.reshape(-1)

    def of_chip(token):
        mine = lax.dynamic_slice_in_dim(token, device * rows, rows)
        other = lax.dynamic_slice_in_dim(token, (device ^ 1) * rows, rows)
        return jnp.concatenate([mine, other])

    bwd_token = tokens_of(starts[2], starts[3])
    own_rank = lax.dynamic_slice_in_dim(starts[4], device * owned, owned)
    column = jnp.arange(owned * rank, dtype=jnp.int32)
    row = jnp.arange(rows, dtype=jnp.int32)
    factor = jnp.repeat(8.0 / jnp.sqrt(own_rank.astype(F32)), rank)
    live = column % rank < jnp.repeat(own_rank, rank)
    mine = row[:, None] // window == column[None, :] // rank
    scale = jnp.where(mine & live[None, :], factor[None, :], 0.0)
    spread = (token_ids[:, None] == of_chip(bwd_token)[None, :]).astype(BF16)
    core_index = core.astype(jnp.int32).reshape(1)

    def chips(pairs):
        second, first = (jnp.array(list(offsets), jnp.int32) for offsets in zip(*pairs))
        z = jnp.where(core == 0, chip_z + second, chip_z + first) % SIDE
        x = jnp.where(core == 0, chip_x + first, chip_x + second) % SIDE
        return jnp.concatenate([z * SIDE + x, core.reshape(1), chip.reshape(1)]).astype(jnp.int32)

    far_blocks = [(2, 2), (2, 1), (2, 3), (2, 0)]
    direct_blocks = [(1, 3), (1, 0), (3, 2), (3, 1)]
    rest_blocks = [(1, 2), (1, 1), (3, 3), (3, 0), (0, 2), (0, 1), (0, 3), (0, 0)]
    order = chips(far_blocks + direct_blocks + rest_blocks)
    arrivals = chips([(s, f) for s in (0, 3, 1, 2) for f in (0, 2, 3, 1)])
    grads = jnp.concatenate([cotangent, other_cotangent], axis=1)

    ready = (grad_windows, scale, spread, grads, order, arrivals)
    grad_windows, scale, spread, grads, order, arrivals = lax.optimization_barrier(ready)
    code_grads = code_grads_of(grad_windows, up, scale)
    own_returned, for_other = returned_of(core_index, code_grads, down)
    returned = (own_returned, send(for_other, OTHER_CORE))

    def partial_sums(order, base, sizes):
        return backward_product(order, base, sizes, grads, weight, other_weight, spread, returned)

    far_up, far_down = partial_sums(order, 0, (2, 2))
    order, far_up, far_down = lax.optimization_barrier((order, far_up, far_down))
    far_up, far_down = send(far_up, SECOND_UP), send(far_down, SECOND_DOWN)
    near_up_b, near_down_a = partial_sums(order, 4, (2, 2))
    order, near_up_b, near_down_a = lax.optimization_barrier((order, near_up_b, near_down_a))
    near_up_b, near_down_a = send(near_up_b, SECOND_UP), send(near_down_a, SECOND_DOWN)
    near_up_a, near_down_b, sums_a, sums_b = partial_sums(order, 8, (2, 2, 2, 2))
    near_up_a = send(add_rounded(near_up_a, far_up), SECOND_UP)
    near_down_b = send(add_rounded(near_down_b, far_down), SECOND_DOWN)

    info_later, _ = lax.optimization_barrier((info, sums_a))
    own_out, for_other_out, own_x, for_other_x = forward_product(
        arrivals, info_later, pieces, weight, other_weight, window, rows
    )
    other_x = send(for_other_x, OTHER_CORE)
    other_out = send(for_other_out, OTHER_CORE)
    codes = forward_codes_of(core_index, own_x, other_x, down, scale)
    leaving = adapter_rows_of(codes, up, devices)
    arrived = lax.all_to_all(leaving, "tp", split_axis=0, concat_axis=0, tiled=True)

    sums_a, sums_b, _ = lax.optimization_barrier((sums_a, sums_b, leaving))
    far_sum = send(add_rounded(sums_a[0], near_up_a[0], near_down_a[0]), FIRST_UP)
    down_sum = send(add_rounded(sums_b[0], near_up_b[0], near_down_b[0]), FIRST_DOWN)
    up_sum = send(add_rounded(sums_a[1], near_up_a[1], near_down_a[1], far_sum), FIRST_UP)
    own_sum = total_of(cotangent, sums_b[1], near_up_b[1], near_down_b[1])
    back_out = add_rounded(own_sum, up_sum, down_sum)
    next_bwd = shifted(back_out, "section", -1)[None]

    layer_out = forward_sum(info, layer_in, own_out, other_out, arrived, window)
    next_fwd = shifted(layer_out, "section", 1)[None]

    back_codes = back_codes_of(stash_windows, down, scale)
    grad_down, grad_up = gradients_of(stash_windows, grad_windows, back_codes, code_grads, owned)
    return (next_fwd, next_bwd, grad_down[None], grad_up[None])


def solution(mesh):
    placed = (
        P("section", None, "tp"),
        P("section", None, "tp"),
        P("section", None, "tp"),
        P("section", None, "tp"),
        P("section", "tp", None, None),
        P("section", "tp", None, None),
        P("section", None),
        P("section", None),
        P(),
        P(),
    )
    return jax.shard_map(
        shards,
        mesh=mesh,
        in_specs=placed,
        out_specs=(
            P("section", None, "tp"),
            P("section", None, "tp"),
            P("section", "tp", None, None),
            P("section", "tp", None, None),
        ),
        check_vma=False,
    )
```

```python
import functools
import math

import jax
import jax.numpy as jnp
from jax import lax
from jax.experimental import pallas as pl
from jax.experimental.pallas import tpu as pltpu
from jax.sharding import PartitionSpec as P

BF16 = jnp.bfloat16
F32 = jnp.float32
SIDE = 4
CHIPS = 16
CORES = 2
BLOCK = 256
SUBLANES = 8
VMEM = 16 * 1024 * 1024


def place(z, x, core):
    return (z * SIDE + x) * CORES + core


def ring_pairs(first, step):
    pairs = []
    for z in range(SIDE):
        for x in range(SIDE):
            for core in range(CORES):
                along_x = (core == 0) == first
                target = place(z, (x + step) % SIDE, core) if along_x else place((z + step) % SIDE, x, core)
                pairs.append((place(z, x, core), target))
    return pairs


FIRST_UP, FIRST_DOWN = ring_pairs(True, 1), ring_pairs(True, -1)
SECOND_UP, SECOND_DOWN = ring_pairs(False, 1), ring_pairs(False, -1)
OTHER_CORE = [(index, index ^ 1) for index in range(CHIPS * CORES)]


def send(value, pairs):
    return lax.ppermute(value, "tp", pairs)


def shifted(value, axis, steps):
    count = lax.axis_size(axis)
    pairs = [(source, (source + steps) % count) for source in range(count)]
    return lax.ppermute(value, axis, pairs)


def whole(shape):
    return pl.BlockSpec(shape, lambda *_: (0,) * len(shape))


def kernel(body, name, grid, prefetched, in_specs, outs, flops, scratch=(), vmem=VMEM):
    out_shape = [jax.ShapeDtypeStruct(shape, dtype) for _, shape, dtype in outs]
    size = sum(2 * math.prod(shape) for _, shape, _ in outs)
    return pl.pallas_call(
        body,
        grid_spec=pltpu.PrefetchScalarGridSpec(
            num_scalar_prefetch=prefetched,
            grid=grid,
            in_specs=in_specs,
            out_specs=[spec for spec, _, _ in outs],
            scratch_shapes=list(scratch),
        ),
        out_shape=out_shape,
        compiler_params=pltpu.CompilerParams(vmem_limit_bytes=vmem),
        cost_estimate=pl.CostEstimate(flops=flops, bytes_accessed=2 * size, transcendentals=0),
        name=name,
    )


def slots_body(fwd_ref, bwd_ref, ranks_ref, slot_ref, info_ref):
    adapters = slot_ref.shape[0]

    def step(adapter, starts):
        slot = slot_ref[adapter]
        fwd, bwd = fwd_ref[adapter], bwd_ref[adapter]
        for row, value in enumerate((starts[0], fwd, starts[1], bwd, ranks_ref[adapter])):
            info_ref[row * adapters + slot] = value
        return starts[0] + fwd, starts[1] + bwd

    zero = jnp.int32(0)
    lax.fori_loop(0, adapters, step, (zero, zero))


def slots(forward_counts, backward_counts, ranks, adapter_slot):
    adapters = adapter_slot.shape[0]
    scalars = pl.BlockSpec(memory_space=pltpu.SMEM)
    return pl.pallas_call(
        slots_body,
        in_specs=[scalars] * 4,
        out_specs=scalars,
        out_shape=jax.ShapeDtypeStruct((5 * adapters,), jnp.int32),
        name="slots",
    )(forward_counts[0], backward_counts[0], ranks, adapter_slot)


def slot_rows(ref, start, length, window):
    past = lax.rem(start, SUBLANES)
    size = window + SUBLANES
    rows = ref[pl.ds(pl.multiple_of(start - past, SUBLANES), size), :]
    rows = pltpu.roll(rows, lax.rem(size - past, size), 0)[:window]
    held = lax.broadcasted_iota(jnp.int32, rows.shape, 0) < length
    return jnp.where(held, rows, 0.0).astype(BF16)


def windows_body(adapters, window, each, info_ref, in_ref, out_ref, wide_ref):
    tokens = in_ref.shape[0]
    step = pl.program_id(0)
    owned = out_ref.shape[1] // window

    @pl.when(step == 0)
    def _():
        wide_ref[:tokens] = in_ref[...].astype(F32)

    for index in range(each):
        slot = step * each + index
        rows = slot_rows(wide_ref, info_ref[2 * adapters + slot], info_ref[3 * adapters + slot], window)
        low = index % owned * window
        out_ref[index // owned, low : low + window] = rows


def windows_of(info, values, adapters, window, rows):
    devices = adapters * window // rows
    tokens = values.shape[0]
    each = 16
    owners = each * window // rows
    out = pl.BlockSpec((owners, rows, BLOCK), lambda i, info: (i, 0, 0))
    return kernel(
        functools.partial(windows_body, adapters, window, each),
        "windows",
        (adapters // each,),
        1,
        [whole(values.shape)],
        [(out, (devices, rows, BLOCK), BF16)],
        2 * 10**9,
        [pltpu.VMEM((tokens + window + SUBLANES, BLOCK), F32)],
        3 * VMEM,
    )(info, values)[0]


NT = (((1,), (1,)), ((), ()))
TN = (((0,), (0,)), ((), ()))
GROUP = 8


def lanes(ref, *index):
    return jnp.concatenate([ref[(slot,) + index] for slot in range(ref.shape[0])], axis=1)


def code_grads_body(windows_ref, up_ref, scale_ref, grads_ref, grad_sum):
    step = pl.program_id(0)

    @pl.when(step == 0)
    def _():
        grad_sum[...] = jnp.zeros_like(grad_sum)

    grad = jnp.concatenate([windows_ref[s] for s in range(GROUP)], axis=1)
    up = up_ref[...].reshape(-1, up_ref.shape[2])
    grad_sum[...] += lax.dot_general(grad, up, NT, preferred_element_type=F32)

    @pl.when(step == pl.num_programs(0) - 1)
    def _():
        grads_ref[...] = (grad_sum[...] * scale_ref[...]).astype(BF16)


def code_grads_of(windows, up, scale):
    devices, rows, _ = windows.shape
    owned, rank, _ = up.shape
    shape = scale.shape
    return kernel(
        code_grads_body,
        "code_grads",
        (devices // GROUP,),
        0,
        [
            pl.BlockSpec((GROUP, rows, BLOCK), lambda i: (i, 0, 0)),
            pl.BlockSpec((owned, rank, GROUP * BLOCK), lambda i: (0, 0, i)),
            whole(shape),
        ],
        [(whole(shape), shape, BF16)],
        10**9,
        [pltpu.VMEM(shape, F32)],
        3 * VMEM,
    )(windows, up, scale)[0]


def back_codes_body(windows_ref, down_ref, scale_ref, codes_ref, code_sum):
    step = pl.program_id(0)

    @pl.when(step == 0)
    def _():
        code_sum[...] = jnp.zeros_like(code_sum)

    stash = jnp.concatenate([windows_ref[s] for s in range(GROUP)], axis=1)
    code_sum[...] += jnp.dot(stash, lanes(down_ref), preferred_element_type=F32)

    @pl.when(step == pl.num_programs(0) - 1)
    def _():
        codes_ref[...] = (code_sum[...] * scale_ref[...]).astype(BF16)


def back_codes_of(windows, down, scale):
    devices, rows, _ = windows.shape
    owned, _, rank = down.shape
    shape = scale.shape
    return kernel(
        back_codes_body,
        "back_codes",
        (devices // GROUP,),
        0,
        [
            pl.BlockSpec((GROUP, rows, BLOCK), lambda i: (i, 0, 0)),
            pl.BlockSpec((owned, GROUP * BLOCK, rank), lambda i: (0, i, 0)),
            whole(shape),
        ],
        [(whole(shape), shape, BF16)],
        10**9,
        [pltpu.VMEM(shape, F32)],
    )(windows, down, scale)[0]


def halves(down):
    owned, _, rank = down.shape
    view = down.reshape(owned, CHIPS, CORES, BLOCK, rank)
    shape = (owned, GROUP, 1, BLOCK, rank)
    own = pl.BlockSpec(shape, lambda i, core: (0, i, core[0], 0, 0))
    other = pl.BlockSpec(shape, lambda i, core: (0, i, 1 - core[0], 0, 0))
    return view, own, other


def returned_body(core_ref, grads_ref, own_down_ref, other_down_ref, own_ref, other_ref):
    grads = grads_ref[...]
    for down_ref, out_ref in ((other_down_ref, other_ref), (own_down_ref, own_ref)):
        for index in range(GROUP):
            part = lax.dot_general(grads, lanes(down_ref, index, 0), NT, preferred_element_type=F32)
            out_ref[index] = part.astype(BF16)


def returned_of(core, code_grads, down):
    rows = code_grads.shape[0]
    view, own, other = halves(down)
    out = pl.BlockSpec((GROUP, rows, BLOCK), lambda i, core: (i, 0, 0))
    return kernel(
        returned_body,
        "returned",
        (CHIPS // GROUP,),
        1,
        [whole(code_grads.shape), own, other],
        [(out, (CHIPS, rows, BLOCK), BF16)] * 2,
        10**9,
    )(core, code_grads, view, view)


def forward_codes_body(core_ref, own_x_ref, other_x_ref, own_down_ref, other_down_ref, scale_ref, codes_ref, code_sum):
    step = pl.program_id(0)

    @pl.when(step == 0)
    def _():
        code_sum[...] = jnp.zeros_like(code_sum)

    for x_ref, down_ref in ((own_x_ref, own_down_ref), (other_x_ref, other_down_ref)):
        x = jnp.concatenate([x_ref[s] for s in range(GROUP)], axis=1)
        matrix = jnp.concatenate([lanes(down_ref, s, 0) for s in range(GROUP)], axis=0)
        code_sum[...] += jnp.dot(x, matrix, preferred_element_type=F32)

    @pl.when(step == pl.num_programs(0) - 1)
    def _():
        codes_ref[...] = (code_sum[...] * scale_ref[...]).astype(BF16)


def forward_codes_of(core, own_windows, other_windows, down, scale):
    rows = own_windows.shape[1]
    view, own, other = halves(down)
    x = pl.BlockSpec((GROUP, rows, BLOCK), lambda i, core: (i, 0, 0))
    shape = scale.shape
    return kernel(
        forward_codes_body,
        "forward_codes",
        (CHIPS // GROUP,),
        1,
        [x, x, own, other, whole(shape)],
        [(whole(shape), shape, BF16)],
        10**9,
        [pltpu.VMEM(shape, F32)],
    )(core, own_windows, other_windows, view, view, scale)[0]


def adapter_body(codes_ref, up_ref, out_ref):
    up = up_ref[...].reshape(-1, up_ref.shape[2])
    part = jnp.dot(codes_ref[...], up, preferred_element_type=F32).astype(BF16)
    for index in range(out_ref.shape[0]):
        out_ref[index] = part[:, index * BLOCK : (index + 1) * BLOCK]


def adapter_rows_of(codes, up, devices):
    rows = codes.shape[0]
    owned, rank, _ = up.shape
    out = pl.BlockSpec((GROUP, rows, BLOCK), lambda i: (i, 0, 0))
    return kernel(
        adapter_body,
        "adapter_rows",
        (devices // GROUP,),
        0,
        [whole(codes.shape), pl.BlockSpec((owned, rank, GROUP * BLOCK), lambda i: (0, 0, i))],
        [(out, (devices, rows, BLOCK), BF16)],
        10**9,
    )(codes, up)[0]


def forward_sum_body(window, info_ref, x_ref, own_ref, other_ref, adapter_ref, out_ref, wide_ref):
    tokens = x_ref.shape[0]
    wide_ref[:tokens] = x_ref[...].astype(F32) + (own_ref[...] + other_ref[...])
    devices, rows, _ = adapter_ref.shape
    owned = rows // window
    spare = jnp.zeros((SUBLANES, BLOCK), F32)
    for slot in range(devices * owned):
        start = info_ref[slot]
        past = lax.rem(start, SUBLANES)
        low = slot % owned * window
        added = adapter_ref[slot // owned, low : low + window].astype(F32)
        added = pltpu.roll(jnp.concatenate([added, spare]), past, 0)
        span = pl.ds(pl.multiple_of(start - past, SUBLANES), window + SUBLANES)
        wide_ref[span, :] += added
    out_ref[...] = wide_ref[:tokens].astype(BF16)


def forward_sum(info, layer_in, own_out, other_out, arrived, window):
    devices, rows, _ = arrived.shape
    shape = layer_in.shape
    adapter = pl.BlockSpec((devices, rows, BLOCK), lambda i, info: (0, 0, 0))
    return kernel(
        functools.partial(forward_sum_body, window),
        "forward_sum",
        (1,),
        1,
        [whole(shape), whole(shape), whole(shape), adapter],
        [(whole(shape), shape, BF16)],
        10**8,
        [pltpu.VMEM((shape[0] + window + SUBLANES, BLOCK), F32)],
    )(info, layer_in, own_out, other_out, arrived)[0]


def gradients_body(stash_ref, grad_ref, codes_ref, grads_ref, down_ref, up_ref):
    owned, _, rank = down_ref.shape
    for s in range(GROUP):
        span = slice(s * BLOCK, (s + 1) * BLOCK)
        down = lax.dot_general(stash_ref[s], grads_ref[...], TN, preferred_element_type=F32).astype(BF16)
        up = lax.dot_general(codes_ref[...], grad_ref[s], TN, preferred_element_type=F32).astype(BF16)
        for slot in range(owned):
            own = slice(slot * rank, (slot + 1) * rank)
            down_ref[slot, span] = down[:, own]
            up_ref[slot, :, span] = up[own]


def gradients_of(stash_windows, grad_windows, back_codes, code_grads, owned):
    devices, rows, _ = grad_windows.shape
    rank = back_codes.shape[1] // owned
    width = devices * BLOCK
    return kernel(
        gradients_body,
        "gradients",
        (devices // GROUP,),
        0,
        [
            pl.BlockSpec((GROUP, rows, BLOCK), lambda i: (i, 0, 0)),
            pl.BlockSpec((GROUP, rows, BLOCK), lambda i: (i, 0, 0)),
            whole(back_codes.shape),
            whole(code_grads.shape),
        ],
        [
            (pl.BlockSpec((owned, GROUP * BLOCK, rank), lambda i: (0, i, 0)), (owned, width, rank), BF16),
            (pl.BlockSpec((owned, rank, GROUP * BLOCK), lambda i: (0, 0, i)), (owned, rank, width), BF16),
        ],
        2 * 10**9,
    )(stash_windows, grad_windows, back_codes, code_grads)


PAIR = 2


def forward_body(window, order_ref, info_ref, *rest):
    pieces, rest = rest[:12], rest[12:]
    own_w, other_w, rest = rest[:PAIR], rest[PAIR : 2 * PAIR], rest[2 * PAIR :]
    own_ref, other_ref, own_x_ref, other_x_ref, wide_ref = rest
    step = pl.program_id(0)
    tokens = own_ref.shape[0]
    core = order_ref[CHIPS]
    chip = order_ref[CHIPS + 1]
    adapters = info_ref.shape[0] // 5
    owned = own_x_ref.shape[1] // window

    @pl.when(step == 0)
    def _():
        own_ref[...] = jnp.zeros_like(own_ref)
        other_ref[...] = jnp.zeros_like(other_ref)

    def take(*blocks):
        own_sum, other_sum = own_ref[...], other_ref[...]
        for index, (x_ref, at) in enumerate(blocks):
            x = x_ref[...] if at is None else x_ref[at]
            own_sum += jnp.dot(x, own_w[index][0, 0], preferred_element_type=F32)
            other_sum += jnp.dot(x, other_w[index][0], preferred_element_type=F32)
            wide_ref[:tokens] = x.astype(F32)
            at = order_ref[PAIR * step + index]
            for whose, out_ref in ((core, own_x_ref), (1 - core, other_x_ref)):
                for slot in range(owned):
                    place_of = (chip * CORES + whose) * owned + slot
                    rows = slot_rows(wide_ref, info_ref[place_of], info_ref[adapters + place_of], window)
                    out_ref[at, slot * window : (slot + 1) * window] = rows
        own_ref[...] = own_sum
        other_ref[...] = other_sum

    own, far, near = pieces[0::3], pieces[1::3], pieces[2::3]
    pairs = []
    for line in range(SIDE):
        pairs += [((own[line], None), (far[line], None)), ((near[line], 0), (near[line], 1))]
    for index, pair in enumerate(pairs):
        pl.when(step == index)(functools.partial(take, *pair))


def forward_product(order, info, pieces, weight, other_weight, window, rows):
    tokens = pieces[0].shape[0]
    product = (whole((tokens, BLOCK)), (tokens, BLOCK), F32)
    windows = (whole((CHIPS, rows, BLOCK)), (CHIPS, rows, BLOCK), BF16)

    def own(index):
        shape = (1, 1, BLOCK, BLOCK)
        return pl.BlockSpec(shape, lambda k, order, info: (order[PAIR * k + index], order[CHIPS], 0, 0))

    def other(index):
        return pl.BlockSpec((1, BLOCK, BLOCK), lambda k, order, info: (order[PAIR * k + index], 0, 0))

    return kernel(
        functools.partial(forward_body, window),
        "forward_product",
        (CHIPS // PAIR,),
        2,
        [whole(piece.shape) for piece in pieces]
        + [own(index) for index in range(PAIR)]
        + [other(index) for index in range(PAIR)],
        [product, product, windows, windows],
        9 * 10**9,
        [pltpu.VMEM((tokens + window + SUBLANES, BLOCK), F32)],
    )(order, info, *pieces, *[weight] * PAIR, *[other_weight] * PAIR)


def backward_body(sizes, order_ref, grad_ref, own_w_ref, other_w_ref, spread_ref, own_ret_ref, other_ret_ref, *outs):
    step = pl.program_id(0)
    matrix = jnp.concatenate([own_w_ref[0, 0], other_w_ref[0]], axis=1)
    returned = jnp.concatenate([own_ret_ref[0], other_ret_ref[0]], axis=0)
    total = lax.dot_general(grad_ref[...], matrix, NT, preferred_element_type=F32)
    total += jnp.dot(spread_ref[...], returned, preferred_element_type=F32)
    total = total.astype(BF16)
    low = 0
    for out_ref, size in zip(outs, sizes):

        @pl.when((step >= low) & (step < low + size))
        def _(out_ref=out_ref):
            out_ref[0] = total

        low += size


def backward_product(order, base, sizes, grads, weight, other_weight, spread, returned):
    tokens = grads.shape[0]
    blocks = sum(sizes)

    def out(index):
        low, size = sum(sizes[:index]), sizes[index]
        return pl.BlockSpec((1, tokens, BLOCK), lambda j, order: (jnp.clip(j - low, 0, size - 1), 0, 0))

    rows = pl.BlockSpec((1,) + returned[0].shape[1:], lambda j, order: (order[base + j], 0, 0))
    return kernel(
        functools.partial(backward_body, sizes),
        "backward_product",
        (blocks,),
        1,
        [
            whole(grads.shape),
            pl.BlockSpec((1, 1, BLOCK, BLOCK), lambda j, order: (order[base + j], order[CHIPS], 0, 0)),
            pl.BlockSpec((1, BLOCK, BLOCK), lambda j, order: (order[base + j], 0, 0)),
            whole(spread.shape),
            rows,
            rows,
        ],
        [(out(index), (size, tokens, BLOCK), BF16) for index, size in enumerate(sizes)],
        blocks * 34 * 10**7,
    )(order, grads, weight, other_weight, spread, *returned)


def total_of(*values):
    total = values[0].astype(F32)
    for value in values[1:]:
        total = total + value.astype(F32)
    return total


def add_rounded(*values):
    return total_of(*values).astype(BF16)


def shards(
    forward_inputs,
    backward_inputs,
    backward_cotangents,
    frozen_weight,
    adapter_down_weight,
    adapter_up_weight,
    forward_counts,
    backward_counts,
    ranks,
    adapter_slot,
):
    tokens = forward_inputs.shape[1]
    adapters = adapter_slot.shape[0]
    owned = adapter_down_weight.shape[1]
    rank = adapter_down_weight.shape[3]
    window = 2 * tokens // adapters
    rows = owned * window
    devices = CHIPS * CORES
    device = lax.axis_index("tp")
    core = device % CORES
    chip = device // CORES
    chip_z, chip_x = chip // SIDE, chip % SIDE

    layer_in = forward_inputs[0]
    stash = backward_inputs[0]
    cotangent = backward_cotangents[0]
    weight = frozen_weight[0].reshape(CHIPS, CORES, BLOCK, BLOCK)
    down = adapter_down_weight[0]
    up = adapter_up_weight[0]

    below, above = send(layer_in, FIRST_UP), send(layer_in, FIRST_DOWN)
    own_below, own_above = send(layer_in, SECOND_UP), send(layer_in, SECOND_DOWN)
    far = send(below, FIRST_UP)
    near = jnp.stack([below, above])
    near_below, near_above = send(near, SECOND_UP), send(near, SECOND_DOWN)
    far_below, far_above = send(far, SECOND_UP), send(far, SECOND_DOWN)
    own_far = send(own_above, SECOND_DOWN)
    near_far = send(near_below, SECOND_UP)
    far_far = send(far_above, SECOND_DOWN)
    pieces = (layer_in, far, near, own_below, far_below, near_below, own_above, far_above, near_above)
    pieces += (own_far, far_far, near_far)

    for_other = lax.dynamic_index_in_dim(weight, 1 - core, axis=1, keepdims=False)
    other_weight = send(for_other, OTHER_CORE)
    other_cotangent = send(cotangent, OTHER_CORE)

    info = slots(forward_counts, backward_counts, ranks, adapter_slot)
    grad_windows = windows_of(info, cotangent, adapters, window, rows)
    grad_windows = lax.all_to_all(grad_windows, "tp", split_axis=0, concat_axis=0, tiled=True)

    stash_windows = windows_of(info, stash, adapters, window, rows)
    stash_windows, other_weight = lax.optimization_barrier((stash_windows, other_weight))
    stash_windows = lax.all_to_all(stash_windows, "tp", split_axis=0, concat_axis=0, tiled=True)

    starts = info.reshape(5, adapters)
    offsets = jnp.arange(window, dtype=jnp.int32)
    token_ids = jnp.arange(tokens, dtype=jnp.int32)

    def tokens_of(start, length):
        token = jnp.where(offsets[None, :] < length[:, None], start[:, None] + offsets[None, :], -1)
        return token.reshape(-1)

    def of_chip(token):
        mine = lax.dynamic_slice_in_dim(token, device * rows, rows)
        other = lax.dynamic_slice_in_dim(token, (device ^ 1) * rows, rows)
        return jnp.concatenate([mine, other])

    bwd_token = tokens_of(starts[2], starts[3])
    own_rank = lax.dynamic_slice_in_dim(starts[4], device * owned, owned)
    column = jnp.arange(owned * rank, dtype=jnp.int32)
    row = jnp.arange(rows, dtype=jnp.int32)
    factor = jnp.repeat(8.0 / jnp.sqrt(own_rank.astype(F32)), rank)
    live = column % rank < jnp.repeat(own_rank, rank)
    mine = row[:, None] // window == column[None, :] // rank
    scale = jnp.where(mine & live[None, :], factor[None, :], 0.0)
    spread = (token_ids[:, None] == of_chip(bwd_token)[None, :]).astype(BF16)
    core_index = core.astype(jnp.int32).reshape(1)

    def chips(pairs):
        second, first = (jnp.array(list(offsets), jnp.int32) for offsets in zip(*pairs))
        z = jnp.where(core == 0, chip_z + second, chip_z + first) % SIDE
        x = jnp.where(core == 0, chip_x + first, chip_x + second) % SIDE
        return jnp.concatenate([z * SIDE + x, core.reshape(1), chip.reshape(1)]).astype(jnp.int32)

    far_blocks = [(2, 2), (2, 1), (2, 3), (2, 0)]
    direct_blocks = [(1, 3), (1, 0), (3, 2), (3, 1)]
    rest_blocks = [(1, 2), (1, 1), (3, 3), (3, 0), (0, 2), (0, 1), (0, 3), (0, 0)]
    order = chips(far_blocks + direct_blocks + rest_blocks)
    arrivals = chips([(s, f) for s in (0, 3, 1, 2) for f in (0, 2, 3, 1)])
    grads = jnp.concatenate([cotangent, other_cotangent], axis=1)

    ready = (grad_windows, scale, spread, grads, order, arrivals)
    grad_windows, scale, spread, grads, order, arrivals = lax.optimization_barrier(ready)
    code_grads = code_grads_of(grad_windows, up, scale)
    own_returned, for_other = returned_of(core_index, code_grads, down)
    returned = (own_returned, send(for_other, OTHER_CORE))

    def partial_sums(order, base, sizes):
        return backward_product(order, base, sizes, grads, weight, other_weight, spread, returned)

    far_up, far_down = partial_sums(order, 0, (2, 2))
    order, far_up, far_down = lax.optimization_barrier((order, far_up, far_down))
    far_up, far_down = send(far_up, SECOND_UP), send(far_down, SECOND_DOWN)
    near_up_b, near_down_a = partial_sums(order, 4, (2, 2))
    order, near_up_b, near_down_a = lax.optimization_barrier((order, near_up_b, near_down_a))
    near_up_b, near_down_a = send(near_up_b, SECOND_UP), send(near_down_a, SECOND_DOWN)
    near_up_a, near_down_b, sums_a, sums_b = partial_sums(order, 8, (2, 2, 2, 2))
    near_up_a = send(add_rounded(near_up_a, far_up), SECOND_UP)
    near_down_b = send(add_rounded(near_down_b, far_down), SECOND_DOWN)

    info_later, _ = lax.optimization_barrier((info, sums_a))
    own_out, for_other_out, own_x, for_other_x = forward_product(
        arrivals, info_later, pieces, weight, other_weight, window, rows
    )
    other_x = send(for_other_x, OTHER_CORE)
    other_out = send(for_other_out, OTHER_CORE)
    codes = forward_codes_of(core_index, own_x, other_x, down, scale)
    leaving = adapter_rows_of(codes, up, devices)
    arrived = lax.all_to_all(leaving, "tp", split_axis=0, concat_axis=0, tiled=True)

    sums_a, sums_b, _ = lax.optimization_barrier((sums_a, sums_b, leaving))
    far_sum = send(add_rounded(sums_a[0], near_up_a[0], near_down_a[0]), FIRST_UP)
    down_sum = send(add_rounded(sums_b[0], near_up_b[0], near_down_b[0]), FIRST_DOWN)
    up_sum = send(add_rounded(sums_a[1], near_up_a[1], near_down_a[1], far_sum), FIRST_UP)
    own_sum = total_of(cotangent, sums_b[1], near_up_b[1], near_down_b[1])
    back_out = add_rounded(own_sum, up_sum, down_sum)
    next_bwd = shifted(back_out, "section", -1)[None]

    layer_out = forward_sum(info, layer_in, own_out, other_out, arrived, window)
    next_fwd = shifted(layer_out, "section", 1)[None]

    back_codes = back_codes_of(stash_windows, down, scale)
    grad_down, grad_up = gradients_of(stash_windows, grad_windows, back_codes, code_grads, owned)
    return (next_fwd, next_bwd, grad_down[None], grad_up[None])


def solution(mesh):
    placed = (
        P("section", None, "tp"),
        P("section", None, "tp"),
        P("section", None, "tp"),
        P("section", None, "tp"),
        P("section", "tp", None, None),
        P("section", "tp", None, None),
        P("section", None),
        P("section", None),
        P(),
        P(),
    )
    return jax.shard_map(
        shards,
        mesh=mesh,
        in_specs=placed,
        out_specs=(
            P("section", None, "tp"),
            P("section", None, "tp"),
            P("section", "tp", None, None),
            P("section", "tp", None, None),
        ),
        check_vma=False,
    )
```
